512 devices in a mesh: cluster: 32 (over z_hi, x, core), blk: 16 (over y, z_lo).
Axes of the slice: x: 4, y: 8, z: 8 (z_hi: 4, z_lo: 2; z = z_hi * 2 + z_lo), core: 2. Of those that a mesh axis runs over, the one named last changes fastest.
Arguments:
- coeff: bfloat16 [1024, 8, 2048], P('cluster', None, 'blk'), may hold values from -0.375 to 0.375
- intersection: int32 [32, 32], replicated, may hold values from 0 to 1023, as said below
- basis_vals: bfloat16 [131072, 256], P(('cluster', 'blk')), may hold values from -6 to 6
- coulomb: bfloat16 [131072, 7, 256], P(('cluster', 'blk')), may hold values from -0.125 to 0.125
- reach: int32 [512], P(('cluster', 'blk')), may hold values from 0 to 3, as said below
Outputs:
- exchange_out: bfloat16 [131072, 2048], P(('cluster', 'blk'))
The draws below stay inside these ranges and needn't reach their ends.
Inputs may be any that keep to these rules, and one draw needn't show every extreme that they name: `intersection`: each row lists 32 distinct atoms; atom a is owned by cluster a // 32; at most 2 atoms of one row have the same owner, and each row c holds exactly 2 atoms owned by cluster c. `reach`: some block reaches 3 and some block reaches 0.
All inputs are finite; a program needn't handle non-finite values.
Results may differ from the reference program's by a relative error of at most 0.0059.
Values may be sent and summed in bfloat16 or wider, within the bound.
A program may use at most 64 MiB of HBM per device.

```python
import jax
import jax.numpy as jnp
from jax import lax

NORB = 2048
NAO = 8
NEED = 32
HALF_STOPS = 3
PTS_DEV = 256
ATOM_CL = 32
STOPS = 7
SLOT = 2
NCLUST = 32
BLOCKS = 512
NPTS = 131072
ATOMS = 1024
N_BLK = 16


def draw_intersection(key, part):
    total_slots = NCLUST * SLOT

    def one_row(cluster_id):
        row_key = jax.random.fold_in(jax.random.fold_in(key, 4101), cluster_id)
        shuffled = jax.random.permutation(jax.random.fold_in(row_key, 1), total_slots)
        owners = shuffled // SLOT
        priority = jnp.where(owners == cluster_id, 0, 1) * total_slots + jnp.arange(total_slots, dtype=jnp.int32)
        ranking = jnp.argsort(priority)
        chosen = shuffled[ranking][:NEED]
        chosen = chosen[jax.random.permutation(jax.random.fold_in(row_key, 2), NEED)]
        chosen_owner = chosen // SLOT
        slot_pos = chosen % SLOT
        offsets = jax.random.randint(jax.random.fold_in(row_key, 3), (NCLUST,), 0, ATOM_CL)
        return chosen_owner * ATOM_CL + (slot_pos + offsets[chosen_owner]) % ATOM_CL
    rows = jax.vmap(one_row)(jnp.arange(NCLUST, dtype=jnp.int32))
    return rows.astype(jnp.int32)


def draw_reach(key, part):
    base_key = jax.random.fold_in(key, 7303)
    ranges = jax.random.randint(jax.random.fold_in(base_key, 1), (BLOCKS,), 0, HALF_STOPS + 1)
    shuffled = jax.random.permutation(jax.random.fold_in(base_key, 2), BLOCKS)
    ranges = ranges.at[shuffled[0]].set(HALF_STOPS)
    ranges = ranges.at[shuffled[1]].set(0)
    return ranges.astype(jnp.int32)


def block_levels(own_key, dims, split, smallest, high):
    level = 1.0
    for axis_at, parts in split:
        draws = jax.random.uniform(jax.random.fold_in(jax.random.fold_in(own_key, 6), axis_at), (parts,), jnp.float32, smallest / len(split), high / len(split))
        level = level * jnp.repeat(jnp.exp(draws), dims[axis_at] // parts).reshape((-1,) + (1,) * (len(dims) - 1 - axis_at))
    return level


def scatter_about(own_key, shape, deviation, bound, cuts=(), held_as=jnp.bfloat16):
    array = jax.random.normal(own_key, shape, jnp.float32) * deviation
    if len(cuts) > 0:
        array = block_levels(own_key, shape, cuts, -0.22, 0.18) * array
    return jnp.clip(array, min=-bound, max=bound).astype(held_as)


def setup_inputs(seed: int = 0) -> dict:
    keys = jax.random.split(jax.random.key(seed), 6)
    return {
        "coeff": scatter_about(keys[0], (ATOMS, NAO, NORB), (NEED * NAO) ** -0.5, 0.375, ((0, 32), (2, 16))),
        "intersection": draw_intersection(jax.random.fold_in(keys[5], 71), 0),
        "basis_vals": scatter_about(keys[2], (NPTS, NEED * NAO), 1.0, 6.0, ((0, 512),)),
        "coulomb": scatter_about(keys[3], (NPTS, STOPS, PTS_DEV), (STOPS * PTS_DEV) ** -0.5, 0.125, ((0, 512),)),
        "reach": draw_reach(jax.random.fold_in(keys[5], 71), 0),
    }


def reference(coeff, intersection, basis_vals, coulomb, reach):
    num_clusters = intersection.shape[0]
    half_stops = (coulomb.shape[1] - 1) // 2
    norm_factor = NORB ** -0.5

    def orbit(cluster_id):
        coeff_rows = coeff[intersection[cluster_id]].reshape(NEED * NAO, NORB)
        basis_block = lax.dynamic_slice_in_dim(basis_vals, cluster_id * (N_BLK * PTS_DEV), N_BLK * PTS_DEV, 0)
        return jnp.dot(basis_block, coeff_rows, preferred_element_type=jnp.float32).astype(jnp.bfloat16)

    orbitals = lax.map(orbit, jnp.arange(num_clusters, dtype=jnp.int32))
    orbitals = orbitals.reshape(num_clusters, N_BLK, PTS_DEV, NORB)
    coul_blocks = coulomb.reshape(num_clusters, N_BLK, PTS_DEV, coulomb.shape[1], PTS_DEV)
    reach_blocks = reach.reshape(num_clusters, N_BLK)

    def one_block(block_id):
        cluster_id = block_id // N_BLK
        blk_id = block_id % N_BLK
        local_vals = orbitals[cluster_id, blk_id]
        accumulated = jnp.zeros((PTS_DEV, NORB), jnp.float32)
        for offset in range(-half_stops, half_stops + 1):
            source_id = (blk_id + offset) % N_BLK
            source = orbitals[cluster_id, source_id]
            density = lax.dot_general(local_vals, source, (((1,), (1,)), ((), ())), preferred_element_type=jnp.float32) * norm_factor
            within = abs(offset) <= reach_blocks[cluster_id, blk_id]
            masked_tile = jnp.where(within, density * coul_blocks[cluster_id, blk_id, :, offset + half_stops, :].astype(jnp.float32), jnp.float32(0.0)).astype(jnp.bfloat16)
            accumulated = accumulated + jnp.dot(masked_tile, source, preferred_element_type=jnp.float32)
        return accumulated.astype(jnp.bfloat16)

    result = lax.map(one_block, jnp.arange(num_clusters * N_BLK, dtype=jnp.int32))
    return result.reshape(NPTS, NORB)
```

```python
import jax
import jax.numpy as jnp
from jax import lax
from jax.experimental import pallas as pl
from jax.experimental.pallas import tpu as pltpu
from jax.sharding import PartitionSpec as P

MESH = pl.DeviceIdType.MESH
F32 = jnp.float32
BF16 = jnp.bfloat16

YP, YM, ZZ = 0, 1, 2

PART, UP, DOWN, PART_UP, PART_DOWN, PART_DOWN2 = range(6)
SLOT_OFFSET = {PART: 1, UP: 2, DOWN: -2, PART_UP: 3, PART_DOWN: -1, PART_DOWN2: -3}

GATHER = [
    (ZZ, 0, 0, 0), (YP, 0, 0, 0), (YM, 0, 0, 0),
    (ZZ, 0, 0, 1), (YP, 0, 0, 1), (YM, 0, 0, 1),
    "basis",
    (YP, 0, -1, 0), (YM, 0, 1, 0), (ZZ, 0, -1, 0), (ZZ, 0, 1, 0),
    (YP, 0, -1, 1), (YM, 0, 1, 1), (ZZ, 0, -1, 1), (ZZ, 0, 1, 1),
    "fold0",
    (YP, 0, -2, 0), (YM, 0, 2, 0),
    (YP, 1, -1, 0), (YM, 1, 1, 0),
    (YP, 0, -2, 1), (YM, 0, 2, 1),
    (YP, 1, -1, 1), (YM, 1, 1, 1),
    "basis2",
    "fold1",
    (YP, 0, -3, 0), (YM, 0, 3, 1), (ZZ, 0, -3, 1), (ZZ, 0, 3, 0),
    (YP, 1, -2, 0), (YM, 1, 2, 1),
    "fold2",
    (ZZ, 0, 4, 0), (ZZ, 0, 4, 1),
    "fold3",
]
SENDS = [s for s in GATHER if not isinstance(s, str)]


def arrivals():
    count = {YP: 0, YM: 0, ZZ: 0}
    index, came = {}, {}
    for link, plane, dist, half in SENDS:
        k = count[link]
        count[link] += 1
        index[(link, plane, dist, half)] = k
        if link == ZZ:
            seen = (1 - plane, dist, half)
        else:
            step = -1 if link == YP else 1
            seen = (plane, dist + step, half)
        if abs(seen[1]) == 4:
            seen = (seen[0], 4, seen[2])
        assert seen not in came and seen != (0, 0, 0)
        came[seen] = (link, k)
    return index, came


INDEX, CAME = arrivals()


def gather_kernel(
    n_y, n_clust, coeff_ref, inter_ref, basis_ref, coul_hbm, reach_ref,
    n_out, w_out,
    coul_v, coul_f, coul_t, out_buf, in_buf, n_buf, b_buf, g_ref,
    coul_sem, nout_sem, a2a_send, a2a_recv, b_send, b_recv, ag_send, ag_recv,
):
    c = lax.axis_index("cluster")
    b = lax.axis_index("blk")
    y, z = b // 2, b % 2
    sign = 1 - 2 * z
    rows = basis_ref.shape[0]
    stops = coul_v.shape[1]
    half_stops = (stops - 1) // 2

    def at(yy, zz):
        return lax.rem(yy + 2 * n_y, n_y) * 2 + zz

    link_to = {YP: at(y + 1, z), YM: at(y - 1, z), ZZ: at(y, 1 - z)}

    coul_copy = pltpu.make_async_copy(coul_hbm, coul_v, coul_sem)
    coul_copy.start()

    barrier = pltpu.get_barrier_semaphore()

    def greet(i, _):
        pl.semaphore_signal(
            barrier, inc=1, device_id=(lax.rem(c + i, n_clust), b), device_id_type=MESH
        )
        return 0

    lax.fori_loop(1, n_clust, greet, 0)
    for link in (YP, YM, ZZ):
        pl.semaphore_signal(barrier, inc=1, device_id=(c, link_to[link]), device_id_type=MESH)

    inter = inter_ref[...]
    n_list = inter.shape[1]
    n_atoms = 32
    slot_rows = 16 * n_clust
    owner = inter // n_atoms
    local = inter - owner * n_atoms
    mine = (owner == c).astype(F32)
    tri = (
        lax.broadcasted_iota(jnp.int32, (n_list, n_list), 0)
        < lax.broadcasted_iota(jnp.int32, (n_list, n_list), 1)
    ).astype(F32)
    rank = jnp.dot(mine, tri, preferred_element_type=F32)
    spread = (
        lax.broadcasted_iota(jnp.int32, (slot_rows, n_clust), 0) // 16
        == lax.broadcasted_iota(jnp.int32, (slot_rows, n_clust), 1)
    ).astype(F32)
    mine_e = jnp.dot(spread, mine, preferred_element_type=F32)
    rank_e = jnp.dot(spread, rank, preferred_element_type=F32)
    local_e = jnp.dot(spread, local.astype(F32), preferred_element_type=F32)
    row = lax.broadcasted_iota(jnp.int32, (slot_rows, 1), 0)
    slot = ((row // 8) % 2).astype(F32)
    func = (row % 8).astype(F32)
    take = mine_e * (rank_e == slot).astype(F32)
    filled = jnp.sum(take, axis=1, keepdims=True)
    source = jnp.sum(take * local_e, axis=1, keepdims=True) * 8 + func
    source = jnp.where(filled > 0.5, source, -1.0)
    pick = (
        lax.broadcasted_iota(jnp.int32, (slot_rows, rows), 1).astype(F32) == source
    ).astype(BF16)
    coeff = coeff_ref[...].astype(F32).reshape(rows, coeff_ref.shape[2]).astype(BF16)
    out_buf[...] = jnp.dot(pick, coeff, preferred_element_type=F32).astype(BF16)

    pl.semaphore_wait(barrier, n_clust - 1 + 3)

    def a2a(i):
        to = lax.rem(c + i, n_clust)
        return pltpu.make_async_remote_copy(
            src_ref=out_buf.at[pl.ds(pl.multiple_of(to * 16, 16), 16)],
            dst_ref=in_buf.at[pl.ds(pl.multiple_of(c * 16, 16), 16)],
            send_sem=a2a_send.at[i],
            recv_sem=a2a_recv.at[i],
            device_id=(to, b),
            device_id_type=MESH,
        )

    def a2a_start(i, _):
        a2a(i).start()
        return 0

    lax.fori_loop(1, n_clust, a2a_start, 0)

    up = at(y + sign, z)
    down = at(y - sign, z)
    across = link_to[ZZ]

    def basis_copy(src, slot_at, k, to):
        return pltpu.make_async_remote_copy(
            src_ref=basis_ref if src is None else b_buf.at[src],
            dst_ref=b_buf.at[slot_at],
            send_sem=b_send.at[k],
            recv_sem=b_recv.at[slot_at],
            device_id=(c, to),
            device_id_type=MESH,
        )

    basis_sends = [
        basis_copy(None, PART, 0, across),
        basis_copy(None, DOWN, 1, up),
        basis_copy(None, UP, 2, down),
        basis_copy(PART, PART_UP, 3, down),
        basis_copy(UP, PART_DOWN, 4, across),
        basis_copy(PART_DOWN, PART_DOWN2, 5, up),
    ]
    got_basis = set()

    def need_basis(slot_at):
        if slot_at not in got_basis:
            got_basis.add(slot_at)
            next(s for s, k in zip(basis_sends, (PART, DOWN, UP, PART_UP, PART_DOWN, PART_DOWN2)) if k == slot_at).wait_recv()

    for k in range(3):
        basis_sends[k].start()

    own_list = inter_ref[pl.ds(c, 1), :]
    own_owner = (own_list // n_atoms).astype(F32)
    entry = lax.broadcasted_iota(jnp.int32, (rows, n_list), 0) // 8
    column = lax.broadcasted_iota(jnp.int32, (rows, n_list), 1)
    own_row = jnp.broadcast_to(own_owner, (rows, n_list))
    owner_col = jnp.sum(jnp.where(entry == column, own_row, 0.0), axis=1, keepdims=True)
    own_rank = jnp.sum(
        jnp.where((own_row == owner_col) & (column < entry), 1.0, 0.0), axis=1, keepdims=True
    )
    func_col = (lax.broadcasted_iota(jnp.int32, (rows, 1), 0) % 8).astype(F32)
    place = owner_col * 16 + own_rank * 8 + func_col
    unpack = (
        lax.broadcasted_iota(jnp.int32, (rows, slot_rows), 1).astype(F32) == place
    ).astype(BF16)
    own_at = pl.ds(pl.multiple_of(c * 16, 16), 16)
    in_buf[own_at, :] = out_buf[own_at, :]

    coul_copy.wait()
    part = 32

    def widen(i, _):
        at_rows = pl.ds(pl.multiple_of(i * part, part), part)
        wide = coul_v[at_rows].astype(F32)
        for side in range(rows // 128):
            coul_f[side, at_rows, 0:stops, :] = wide[:, :, side * 128 : (side + 1) * 128]
        return 0

    lax.fori_loop(0, rows // part, widen, 0)

    def a2a_wait(i, _):
        a2a(i).wait_recv()
        return 0

    lax.fori_loop(1, n_clust, a2a_wait, 0)
    chunk = jnp.dot(unpack, in_buf[...], preferred_element_type=F32)
    n_buf[b] = chunk.astype(BF16)

    def chunk_at(plane, dist):
        return at(y + dist, z if plane == 0 else 1 - z)

    half = rows // 2

    def gather(link, plane, dist, h):
        k = INDEX[(link, plane, dist, h)]
        where = n_buf.at[chunk_at(plane, dist), pl.ds(h * half, half)]
        return pltpu.make_async_remote_copy(
            src_ref=where,
            dst_ref=where,
            send_sem=ag_send.at[link, k],
            recv_sem=ag_recv.at[link, k],
            device_id=(c, link_to[link]),
            device_id_type=MESH,
        )

    have = {(0, 0, 0), (0, 0, 1)}

    def need(plane, dist, h):
        if abs(dist) == 4:
            dist = 4
        if (plane, dist, h) not in have:
            have.add((plane, dist, h))
            link, k = CAME[(plane, dist, h)]
            where = n_buf.at[chunk_at(plane, dist), pl.ds(h * half, half)]
            pltpu.make_async_remote_copy(
                src_ref=where, dst_ref=where, send_sem=ag_send.at[link, k],
                recv_sem=ag_recv.at[link, k], device_id=(c, link_to[link]), device_id_type=MESH,
            ).wait_recv()

    out_copies = []

    def fold(dist, first=False):
        for plane in (0, 1):
            for h in (0, 1):
                need(plane, dist, h)
        pair = lax.rem(y + dist + 2 * n_y, n_y) * 2
        copy = pltpu.make_async_copy(
            n_buf.at[pl.ds(pair, 2)], n_out.at[pl.ds(pair, 2)], nout_sem.at[len(out_copies)]
        )
        copy.start()
        out_copies.append(copy)
        both = jnp.concatenate([n_buf[pair], n_buf[pair + 1]], axis=1)
        term = lax.dot_general(both, both, (((1,), (1,)), ((), ())), preferred_element_type=F32)
        g_ref[...] = term if first else g_ref[...] + term

    def turn():
        flat = coul_f.reshape(rows // 128, rows * 8, 128)
        reach = reach_ref[0]
        for o in range(stops):
            within = jnp.where(abs(o - half_stops) <= reach, F32(1.0), F32(0.0))
            for side in range(rows // 128):
                tile = flat[side, pl.ds(o, rows, stride=8), :]
                coul_t[o, :, side * 128 : (side + 1) * 128] = tile * within

    for item in GATHER:
        if item == "basis":
            need_basis(PART)
            basis_sends[3].start()
            need_basis(UP)
            basis_sends[4].start()
        elif item == "basis2":
            need_basis(PART_DOWN)
            basis_sends[5].start()
        elif item == "fold0":
            fold(0, True)
            turn()
        elif item == "fold1":
            fold(1)
            fold(-1)
        elif item == "fold2":
            fold(2)
            fold(-2)
        elif item == "fold3":
            for slot_at in SLOT_OFFSET:
                need_basis(slot_at)
            fold(3)
            fold(-3)
            fold(4)
        else:
            need(*item[1:])
            gather(*item).start()

    basis = basis_ref[...]
    scale = (n_out.shape[0] * n_out.shape[2]) ** -0.5
    g = g_ref[...]
    g_hi = g.astype(BF16)
    g_lo = (g - g_hi.astype(F32)).astype(BF16)
    h = jnp.dot(basis, g_hi, preferred_element_type=F32) + jnp.dot(
        basis, g_lo, preferred_element_type=F32
    )
    h = (h * scale).astype(BF16)
    w = None
    for slot_at, offset in [(None, 0)] + list(SLOT_OFFSET.items()):
        other = basis if slot_at is None else b_buf[slot_at]
        density = lax.dot_general(h, other, (((1,), (1,)), ((), ())), preferred_element_type=F32)
        tile = (density * coul_t[half_stops + sign * offset]).astype(BF16)
        term = jnp.dot(tile, other, preferred_element_type=F32)
        w = term if w is None else w + term
    w_out[...] = w.astype(BF16)

    def a2a_sent(i, _):
        a2a(i).wait_send()
        return 0

    lax.fori_loop(1, n_clust, a2a_sent, 0)
    for copy in basis_sends:
        copy.wait_send()
    for item in SENDS:
        gather(*item).wait_send()
    for copy in out_copies:
        copy.wait()


def apply_kernel(w_ref, n_ref, out_ref):
    w = w_ref[...]
    for j in range(n_ref.shape[0] // 2):
        both = jnp.concatenate([n_ref[2 * j], n_ref[2 * j + 1]], axis=1)
        width = both.shape[1]
        out_ref[:, j * width : (j + 1) * width] = jnp.dot(
            w, both, preferred_element_type=F32
        ).astype(BF16)


def solution(mesh):
    n_clust, n_blk = mesh.shape["cluster"], mesh.shape["blk"]

    def on_device(coeff, intersection, basis_vals, coulomb, reach):
        rows, funcs = basis_vals.shape
        columns = coeff.shape[2]
        stops = coulomb.shape[1]
        vmem = pl.BlockSpec(memory_space=pltpu.VMEM)
        anyw = pl.BlockSpec(memory_space=pl.ANY)
        per_link = 10

        def body(*refs):
            gather_kernel(n_blk // 2, n_clust, *refs)

        needed, w = pl.pallas_call(
            body,
            out_shape=(
                jax.ShapeDtypeStruct((n_blk, funcs, columns), BF16),
                jax.ShapeDtypeStruct((rows, funcs), BF16),
            ),
            in_specs=[vmem, vmem, vmem, anyw, pl.BlockSpec(memory_space=pltpu.SMEM)],
            out_specs=(anyw, vmem),
            scratch_shapes=[
                pltpu.VMEM((rows, stops, rows), BF16),
                pltpu.VMEM((rows // 128, rows, 8, 128), F32),
                pltpu.VMEM((stops, rows, rows), F32),
                pltpu.VMEM((16 * n_clust, columns), BF16),
                pltpu.VMEM((16 * n_clust, columns), BF16),
                pltpu.VMEM((n_blk, funcs, columns), BF16),
                pltpu.VMEM((6, rows, funcs), BF16),
                pltpu.VMEM((funcs, funcs), F32),
                pltpu.SemaphoreType.DMA,
                pltpu.SemaphoreType.DMA((8,)),
                pltpu.SemaphoreType.DMA((n_clust,)),
                pltpu.SemaphoreType.DMA((n_clust,)),
                pltpu.SemaphoreType.DMA((6,)),
                pltpu.SemaphoreType.DMA((6,)),
                pltpu.SemaphoreType.DMA((3, per_link)),
                pltpu.SemaphoreType.DMA((3, per_link)),
            ],
            compiler_params=pltpu.CompilerParams(
                collective_id=0, has_side_effects=True, vmem_limit_bytes=48 * 2**20
            ),
            name="gather",
        )(coeff, intersection, basis_vals, coulomb, reach)

        group = 4
        return pl.pallas_call(
            apply_kernel,
            out_shape=jax.ShapeDtypeStruct((rows, n_blk * columns), BF16),
            grid=(n_blk // group,),
            in_specs=[
                pl.BlockSpec((rows, funcs), lambda i: (0, 0)),
                pl.BlockSpec((group, funcs, columns), lambda i: (i, 0, 0)),
            ],
            out_specs=pl.BlockSpec((rows, group * columns), lambda i: (0, i)),
            compiler_params=pltpu.CompilerParams(vmem_limit_bytes=16 * 2**20),
            name="apply",
        )(w, needed)

    return jax.shard_map(
        on_device,
        mesh=mesh,
        in_specs=(
            P("cluster", None, "blk"),
            P(),
            P(("cluster", "blk"), None),
            P(("cluster", "blk"), None, None),
            P(("cluster", "blk")),
        ),
        out_specs=P(("cluster", "blk"), None),
        check_vma=False,
    )
```

```python
import jax
import jax.numpy as jnp
from jax import lax
from jax.experimental import pallas as pl
from jax.experimental.pallas import tpu as pltpu
from jax.sharding import PartitionSpec as P

MESH = pl.DeviceIdType.MESH
F32 = jnp.float32
BF16 = jnp.bfloat16

PART, UP, DOWN, PART_UP, PART_DOWN, PART_DOWN2 = range(6)
SLOT_OFFSET = {PART: 1, UP: 2, DOWN: -2, PART_UP: 3, PART_DOWN: -1, PART_DOWN2: -3}

PARTS = 4
FIRST = [
    (0, 1, 0, 0, 0, 4),
    (2, 0, 0, 0, 0, 4), (-2, 0, 0, 0, 0, 4),
    (1, 0, 0, 0, 0, 4), (-1, 0, 0, 0, 0, 4),
]
THEN = [
    (1, 0, 1, 0, 0, 4), (-1, 0, 1, 0, 0, 4),
    ((0, 0), (1, 0)),
    (2, 0, 0, -2, 0, 2), (-2, 0, 0, 2, 2, 4),
    (1, 0, 0, -2, 0, 4), (-1, 0, 0, 2, 0, 4),
    (0, 1, 0, -2, 0, 4), (0, 1, 0, 2, 0, 4),
    "basis",
    ((0, 1), (0, -1)), ((0, 2), (0, -2)), ((1, 1), (1, -1)),
    (0, 1, 0, 4, 0, 2), (0, 1, 0, 4, 2, 4),
    (0, 1, 0, -3, 0, 4), (0, 1, 0, 3, 0, 4),
    ((0, 3), (0, -3)), ((1, 2), (1, -2)), ((0, 4), (1, 4)), ((1, 3), (1, -3)),
]
SENDS = FIRST + [s for s in THEN if len(s) == 6]


def wrapped(dist):
    return (dist + 3) % 8 - 3


def arrivals():
    came = {}
    for k, (up, across, plane, dist, first, end) in enumerate(SENDS):
        for part in range(first, end):
            key = ((plane + across) % 2, wrapped(dist - up), part)
            assert key not in came and key[:2] != (0, 0)
            came[key] = k
    assert len(came) == 15 * PARTS
    return came


CAME = arrivals()


def at(yy, zz, n_y):
    return lax.rem(yy + 2 * n_y, n_y) * 2 + zz


def exchange(n_y, basis_hbm, blocks, send_sem, recv_sem):
    c = lax.axis_index("cluster")
    b = lax.axis_index("blk")
    y, z = b // 2, b % 2
    sign = 1 - 2 * z
    up, down, across = at(y + sign, z, n_y), at(y - sign, z, n_y), at(y, 1 - z, n_y)

    def copy(src, slot_at, to):
        return pltpu.make_async_remote_copy(
            src_ref=basis_hbm if src is None else blocks.at[src],
            dst_ref=blocks.at[slot_at],
            send_sem=send_sem.at[slot_at],
            recv_sem=recv_sem.at[slot_at],
            device_id=(c, to),
            device_id_type=MESH,
        )

    copies = [
        copy(None, PART, across),
        copy(None, UP, down),
        copy(None, DOWN, up),
        copy(PART, PART_UP, down),
        copy(UP, PART_DOWN, across),
        copy(PART_DOWN, PART_DOWN2, up),
    ]

    def begin():
        for k in (PART, UP, DOWN):
            copies[k].start()

    def relay():
        copies[PART].wait_recv()
        copies[PART_UP].start()
        copies[UP].wait_recv()
        copies[PART_DOWN].start()

    def relay_last():
        copies[PART_DOWN].wait_recv()
        copies[PART_DOWN2].start()

    def finish():
        for k in (DOWN, PART_UP, PART_DOWN2):
            copies[k].wait_recv()
        for k in range(6):
            copies[k].wait_send()

    return begin, relay, relay_last, finish


def gather_kernel(
    n_y, n_clust, coeff_hbm, inter_hbm, basis_hbm, coul_hbm, reach_ref,
    n_buf, w_out,
    coeff_ref, inter_ref, basis_ref, coul_v, coeff_f, out_f, out_buf, in_buf, blocks, g_ref,
    load_sem, a2a_send, a2a_recv, b_send, b_recv, ag_send, ag_recv,
):
    c = lax.axis_index("cluster")
    b = lax.axis_index("blk")
    y, z = b // 2, b % 2
    sign = 1 - 2 * z
    rows = basis_ref.shape[0]
    stops = coul_v.shape[0]
    half_stops = (stops - 1) // 2

    inter_load, coeff_load, basis_load, coul_load = [
        pltpu.make_async_copy(src, dst, load_sem.at[k])
        for k, (src, dst) in enumerate(
            (
                (inter_hbm, inter_ref),
                (coeff_hbm, coeff_ref),
                (basis_hbm, basis_ref),
                (coul_hbm, coul_v),
            )
        )
    ]
    inter_load.start()
    coeff_load.start()

    barrier = pltpu.get_barrier_semaphore()

    def greet(to, _):
        @pl.when(to != c)
        def _():
            pl.semaphore_signal(barrier, inc=1, device_id=(to, b), device_id_type=MESH)

        return 0

    lax.fori_loop(0, n_clust, greet, 0)
    greeted = [(y + d, z) for d in (1, -1, 2, -2)] + [(y, 1 - z)]
    for yy, zz in greeted:
        pl.semaphore_signal(
            barrier, inc=1, device_id=(c, at(yy, zz, n_y)), device_id_type=MESH
        )

    inter_load.wait()
    inter = inter_ref[...]
    n_list = inter.shape[1]
    n_atoms, funcs, columns = coeff_ref.shape
    slot_rows = 2 * funcs * n_clust
    owner = inter // n_atoms
    key = lax.broadcasted_iota(jnp.int32, inter.shape, 1) * n_atoms + (inter - owner * n_atoms)
    key = key.astype(F32)
    top = F32(n_list * n_atoms)
    low = jnp.min(jnp.where(owner == c, key, top), axis=1, keepdims=True)
    high = jnp.max(jnp.where(owner == c, key, -1.0), axis=1, keepdims=True)
    low_at = jnp.where(low < top, low.astype(jnp.int32) % n_atoms, -1)
    high_at = jnp.where(high > low, high.astype(jnp.int32) % n_atoms, -1)
    atom = lax.broadcasted_iota(jnp.int32, (n_clust, n_atoms), 1)
    pick = jnp.concatenate([atom == low_at, atom == high_at], axis=0).astype(F32).astype(BF16)
    coeff_load.wait()
    coeff_f[...] = coeff_ref[...].astype(F32).reshape(n_atoms * funcs, columns)
    by_atom = jnp.concatenate(
        [coeff_f[pl.ds(m, n_atoms, stride=funcs), :].astype(BF16) for m in range(funcs)], axis=1
    )
    packed = jnp.dot(pick, by_atom, preferred_element_type=F32)
    for s in range(2):
        for m in range(funcs):
            out_f[pl.ds(s * funcs + m, n_clust, stride=2 * funcs), :] = packed[
                s * n_clust : (s + 1) * n_clust, m * columns : (m + 1) * columns
            ]
    out_buf[...] = out_f[...].astype(BF16)

    pl.semaphore_wait(barrier, n_clust - 1 + len(greeted))

    def a2a(to, source):
        return pltpu.make_async_remote_copy(
            src_ref=out_buf.at[pl.ds(pl.multiple_of(to * 16, 16), 16)],
            dst_ref=in_buf.at[pl.ds(pl.multiple_of(source * 16, 16), 16)],
            send_sem=a2a_send.at[to],
            recv_sem=a2a_recv.at[source],
            device_id=(to, b),
            device_id_type=MESH,
        )

    def a2a_start(to, _):
        @pl.when(to != c)
        def _():
            a2a(to, c).start()

        return 0

    lax.fori_loop(0, n_clust, a2a_start, 0)
    begin_basis, relay_basis, relay_basis_last, finish_basis = exchange(
        n_y, basis_hbm, blocks, b_send, b_recv
    )
    begin_basis()
    basis_load.start()
    coul_load.start()

    own_list = inter_ref[pl.ds(c, 1), :]
    own_owner = (own_list // n_atoms).astype(F32)
    entry = lax.broadcasted_iota(jnp.int32, (rows, n_list), 0) // funcs
    column = lax.broadcasted_iota(jnp.int32, (rows, n_list), 1)
    own_row = jnp.broadcast_to(own_owner, (rows, n_list))
    owner_col = jnp.sum(jnp.where(entry == column, own_row, 0.0), axis=1, keepdims=True)
    own_rank = jnp.sum(
        jnp.where((own_row == owner_col) & (column < entry), 1.0, 0.0), axis=1, keepdims=True
    )
    func_col = (lax.broadcasted_iota(jnp.int32, (rows, 1), 0) % funcs).astype(F32)
    place = owner_col * (2 * funcs) + own_rank * funcs + func_col
    unpack = (
        lax.broadcasted_iota(jnp.int32, (rows, slot_rows), 1).astype(F32) == place
    ).astype(BF16)
    own_at = pl.ds(pl.multiple_of(c * 16, 16), 16)
    in_buf[own_at, :] = out_buf[own_at, :]

    def a2a_wait(source, _):
        @pl.when(source != c)
        def _():
            a2a(c, source).wait_recv()

        return 0

    lax.fori_loop(0, n_clust, a2a_wait, 0)
    chunk = jnp.dot(unpack, in_buf[...], preferred_element_type=F32)
    n_buf[b] = chunk.astype(BF16)

    def chunk_at(plane, dist):
        return at(y + dist, z if plane == 0 else 1 - z, n_y)

    part_rows = rows // PARTS

    def send(k):
        rise, across, plane, dist, first, end = SENDS[k]
        where = n_buf.at[
            chunk_at(plane, dist), pl.ds(first * part_rows, (end - first) * part_rows)
        ]
        return pltpu.make_async_remote_copy(
            src_ref=where,
            dst_ref=where,
            send_sem=ag_send.at[k],
            recv_sem=ag_recv.at[k],
            device_id=(c, at(y + rise, 1 - z if across else z, n_y)),
            device_id_type=MESH,
        )

    have = set()

    def need(plane, dist, first=0, end=PARTS):
        if (plane, dist) == (0, 0):
            return
        for part in range(first, end):
            k = CAME[(plane, wrapped(dist), part)]
            if k not in have:
                have.add(k)
                send(k).wait_recv()

    for k in range(len(FIRST)):
        send(k).start()
    relay_basis()
    k = len(FIRST)
    folded = False
    for item in THEN:
        if item == "basis":
            relay_basis_last()
        elif len(item) == 6:
            need(*item[2:])
            send(k).start()
            k += 1
        else:
            for chunk_of in item:
                need(*chunk_of)
            both = jnp.concatenate([n_buf[chunk_at(*chunk_of)] for chunk_of in item], axis=1)
            term = lax.dot_general(both, both, (((1,), (1,)), ((), ())), preferred_element_type=F32)
            g_ref[...] = g_ref[...] + term if folded else term
            folded = True
    finish_basis()

    basis_load.wait()
    basis = basis_ref[...]
    scale = (n_buf.shape[0] * n_buf.shape[2]) ** -0.5
    g = g_ref[...]
    g_hi = g.astype(BF16)
    g_lo = (g - g_hi.astype(F32)).astype(BF16)
    h = jnp.dot(basis, g_hi, preferred_element_type=F32) + jnp.dot(
        basis, g_lo, preferred_element_type=F32
    )
    h = (h * scale).astype(BF16)
    coul_load.wait()
    reach = reach_ref[0]
    w = None
    for slot_at, offset in [(None, 0)] + list(SLOT_OFFSET.items()):
        other = basis if slot_at is None else blocks[slot_at]
        density = lax.dot_general(h, other, (((1,), (1,)), ((), ())), preferred_element_type=F32)
        within = jnp.where(abs(offset) <= reach, F32(1.0), F32(0.0))
        coul = coul_v[half_stops + sign * offset].astype(F32) * within
        tile = (density * coul).astype(BF16)
        term = jnp.dot(tile, other, preferred_element_type=F32)
        w = term if w is None else w + term
    w_out[...] = w.astype(BF16)

    def a2a_sent(to, _):
        @pl.when(to != c)
        def _():
            a2a(to, c).wait_send()

        return 0

    lax.fori_loop(0, n_clust, a2a_sent, 0)
    for k in range(len(SENDS)):
        send(k).wait_send()


def apply_kernel(w_ref, n_ref, out_hbm, out_v, sem):
    w = w_ref[...]
    width = 2 * n_ref.shape[2]
    copies = []
    for j in range(n_ref.shape[0] // 2):
        both = jnp.concatenate([n_ref[2 * j], n_ref[2 * j + 1]], axis=1)
        where = slice(j * width, (j + 1) * width)
        out_v[:, where] = jnp.dot(w, both, preferred_element_type=F32).astype(BF16)
        copy = pltpu.make_async_copy(out_v.at[:, where], out_hbm.at[:, where], sem.at[j])
        copy.start()
        copies.append(copy)
    for copy in copies:
        copy.wait()


def solution(mesh):
    n_clust, n_blk = mesh.shape["cluster"], mesh.shape["blk"]
    n_y = n_blk // 2

    def on_device(coeff, intersection, basis_vals, coulomb, reach):
        rows, funcs = basis_vals.shape
        columns = coeff.shape[2]
        stops = coulomb.shape[1]
        vmem = pl.BlockSpec(memory_space=pltpu.VMEM)
        hbm = pl.BlockSpec(memory_space=pltpu.HBM)

        def stay(x):
            return pltpu.with_memory_space_constraint(x, pltpu.HBM)

        basis_vals = stay(basis_vals)

        def gather(*refs):
            gather_kernel(n_y, n_clust, *refs)

        needed, w = pl.pallas_call(
            gather,
            out_shape=(
                jax.ShapeDtypeStruct((n_blk, funcs, columns), BF16),
                jax.ShapeDtypeStruct((rows, funcs), BF16),
            ),
            in_specs=[hbm, hbm, hbm, hbm, pl.BlockSpec(memory_space=pltpu.SMEM)],
            out_specs=(vmem, vmem),
            scratch_shapes=[
                pltpu.VMEM(coeff.shape, BF16),
                pltpu.VMEM(intersection.shape, jnp.int32),
                pltpu.VMEM((rows, funcs), BF16),
                pltpu.VMEM((stops, rows, rows), BF16),
                pltpu.VMEM((coeff.shape[0] * coeff.shape[1], columns), F32),
                pltpu.VMEM((16 * n_clust, columns), F32),
                pltpu.VMEM((16 * n_clust, columns), BF16),
                pltpu.VMEM((16 * n_clust, columns), BF16),
                pltpu.VMEM((6, rows, funcs), BF16),
                pltpu.VMEM((funcs, funcs), F32),
                pltpu.SemaphoreType.DMA((4,)),
                pltpu.SemaphoreType.DMA((n_clust,)),
                pltpu.SemaphoreType.DMA((n_clust,)),
                pltpu.SemaphoreType.DMA((6,)),
                pltpu.SemaphoreType.DMA((6,)),
                pltpu.SemaphoreType.DMA((len(SENDS),)),
                pltpu.SemaphoreType.DMA((len(SENDS),)),
            ],
            compiler_params=pltpu.CompilerParams(
                collective_id=0, has_side_effects=True, vmem_limit_bytes=32 * 2**20
            ),
            name="gather",
        )(
            stay(coeff),
            stay(intersection),
            basis_vals,
            stay(jnp.swapaxes(coulomb, 0, 1)),
            reach,
        )

        return pl.pallas_call(
            apply_kernel,
            out_shape=jax.ShapeDtypeStruct((rows, n_blk * columns), BF16),
            in_specs=[vmem, vmem],
            out_specs=hbm,
            scratch_shapes=[
                pltpu.VMEM((rows, n_blk * columns), BF16),
                pltpu.SemaphoreType.DMA((n_blk // 2,)),
            ],
            compiler_params=pltpu.CompilerParams(vmem_limit_bytes=16 * 2**20),
            name="apply",
        )(w, needed)

    return jax.shard_map(
        on_device,
        mesh=mesh,
        in_specs=(
            P("cluster", None, "blk"),
            P(),
            P(("cluster", "blk"), None),
            P(("cluster", "blk"), None, None),
            P(("cluster", "blk")),
        ),
        out_specs=P(("cluster", "blk"), None),
        check_vma=False,
    )
```

```python
import jax
import jax.numpy as jnp
from jax import lax
from jax.experimental import pallas as pl
from jax.experimental.pallas import tpu as pltpu
from jax.sharding import PartitionSpec as P

MESH = pl.DeviceIdType.MESH
F32 = jnp.float32
BF16 = jnp.bfloat16

PART, UP, DOWN, PART_UP, PART_DOWN, PART_DOWN2 = range(6)
SLOT_OFFSET = {PART: 1, UP: 2, DOWN: -2, PART_UP: 3, PART_DOWN: -1, PART_DOWN2: -3}

GROUPS = 4
PARTS = 4
FIRST = [
    (-1, 0, 0, 0, 2, 4), (1, 0, 0, 0, 2, 4), (0, 1, 0, 0, 0, 2), (-1, 0, 0, 0, 0, 2), (1, 0, 0, 0, 0, 2),
    (-3, 0, 0, 0, 0, 2), (3, 0, 0, 0, 0, 2), (0, 1, 0, 0, 2, 4),
]
THEN = [
    (0, 1, 0, 1, 2, 4), (0, 1, 0, -1, 2, 4), (-2, 0, 0, 1, 2, 4), (2, 0, 0, -1, 2, 4),
    (-1, 0, 0, 1, 2, 4), (1, 0, 0, -1, 2, 4), (0, 1, 0, 1, 0, 2), (0, 1, 0, -1, 0, 2),
    (-1, 0, 0, 1, 0, 2), (1, 0, 0, -1, 0, 2),
    ((0, 0), (1, 0)), ((0, 1), (0, -1)),
    (0, 1, 0, 3, 0, 2), (0, 1, 0, -3, 0, 2), (-1, 0, 1, 1, 2, 4), (1, 0, 1, -1, 2, 4),
    (0, 1, 0, 3, 2, 4), (0, 1, 0, -3, 2, 4), (-1, 1, 0, 3, 0, 2), (1, 1, 0, -3, 2, 4),
    (1, 0, 0, -3, 0, 2), (-1, 0, 0, 3, 2, 4), (-1, 0, 1, 1, 0, 2), (1, 0, 1, -1, 0, 2),
    ((0, 3), (0, -3)), ((1, 1), (1, -1)), ((0, 2), (0, -2)),
    ((1, 2), (1, -2)), ((0, 4), (1, 4)), ((1, 3), (1, -3)),
]
TARGETS = sorted({s[:2] for s in FIRST} | {s[:2] for s in THEN if len(s) == 6})
SENDS = FIRST + [s for s in THEN if len(s) == 6]


def wrapped(dist):
    return (dist + 3) % 8 - 3


def arrivals():
    came = {}
    for k, (up, across, plane, dist, first, end) in enumerate(SENDS):
        for part in range(first, end):
            key = ((plane + across) % 2, wrapped(dist - up), part)
            assert key not in came and key[:2] != (0, 0)
            came[key] = k
    assert len(came) == 15 * PARTS
    return came


CAME = arrivals()


def at(yy, zz, n_y):
    return lax.rem(yy + 2 * n_y, n_y) * 2 + zz


def exchange(n_y, basis_hbm, blocks, send_sem, recv_sem):
    c = lax.axis_index("cluster")
    b = lax.axis_index("blk")
    y, z = b // 2, b % 2
    sign = 1 - 2 * z
    up, down, across = at(y + sign, z, n_y), at(y - sign, z, n_y), at(y, 1 - z, n_y)

    def copy(src, slot_at, to):
        return pltpu.make_async_remote_copy(
            src_ref=basis_hbm if src is None else blocks.at[src],
            dst_ref=blocks.at[slot_at],
            send_sem=send_sem.at[slot_at],
            recv_sem=recv_sem.at[slot_at],
            device_id=(c, to),
            device_id_type=MESH,
        )

    copies = [
        copy(None, PART, across),
        copy(None, UP, down),
        copy(None, DOWN, up),
        copy(PART, PART_UP, down),
        copy(UP, PART_DOWN, across),
        copy(PART_DOWN, PART_DOWN2, up),
    ]

    def begin():
        for k in (PART, UP, DOWN):
            copies[k].start()

    def relay():
        copies[PART].wait_recv()
        copies[PART_UP].start()
        copies[UP].wait_recv()
        copies[PART_DOWN].start()

    def relay_last():
        copies[PART_DOWN].wait_recv()
        copies[PART_DOWN2].start()

    def finish():
        for k in (DOWN, PART_UP, PART_DOWN2):
            copies[k].wait_recv()
        for k in range(6):
            copies[k].wait_send()

    return begin, relay, relay_last, finish


def gather_kernel(
    n_y, n_clust, coeff_hbm, inter_hbm, basis_hbm, coul_hbm, reach_ref,
    n_buf, w_out,
    coeff_ref, inter_ref, basis_ref, coul_v, coeff_f, out_f, out_buf, in_buf, blocks, g_ref,
    load_sem, a2a_send, a2a_recv, b_send, b_recv, ag_send, ag_recv,
):
    c = lax.axis_index("cluster")
    b = lax.axis_index("blk")
    y, z = b // 2, b % 2
    sign = 1 - 2 * z
    rows = basis_ref.shape[0]
    stops = coul_v.shape[0]
    half_stops = (stops - 1) // 2

    inter_load, coeff_load, basis_load, coul_load = [
        pltpu.make_async_copy(src, dst, load_sem.at[k])
        for k, (src, dst) in enumerate(
            (
                (inter_hbm, inter_ref),
                (coeff_hbm, coeff_ref),
                (basis_hbm, basis_ref),
                (coul_hbm, coul_v),
            )
        )
    ]
    inter_load.start()
    coeff_load.start()

    barrier = pltpu.get_barrier_semaphore()

    group = n_clust // GROUPS
    mine = c // group
    first_mate, first_later = mine * group, (mine + 1) * group

    def greet(to, _):
        @pl.when(to != c)
        def _():
            pl.semaphore_signal(barrier, inc=1, device_id=(to, b), device_id_type=MESH)

        return 0

    lax.fori_loop(first_mate, n_clust, greet, 0)
    for rise, across in TARGETS:
        pl.semaphore_signal(
            barrier,
            inc=1,
            device_id=(c, at(y + rise, 1 - z if across else z, n_y)),
            device_id_type=MESH,
        )

    inter_load.wait()
    inter = inter_ref[...]
    n_list = inter.shape[1]
    n_atoms, funcs, columns = coeff_ref.shape
    slot_rows = 2 * funcs * n_clust
    owner = inter // n_atoms
    key = lax.broadcasted_iota(jnp.int32, inter.shape, 1) * n_atoms + (inter - owner * n_atoms)
    key = key.astype(F32)
    top = F32(n_list * n_atoms)
    low = jnp.min(jnp.where(owner == c, key, top), axis=1, keepdims=True)
    high = jnp.max(jnp.where(owner == c, key, -1.0), axis=1, keepdims=True)
    low_at = jnp.where(low < top, low.astype(jnp.int32) % n_atoms, -1)
    high_at = jnp.where(high > low, high.astype(jnp.int32) % n_atoms, -1)
    atom = lax.broadcasted_iota(jnp.int32, (n_clust, n_atoms), 1)
    pick = jnp.concatenate([atom == low_at, atom == high_at], axis=0).astype(F32).astype(BF16)
    coeff_load.wait()
    coeff_f[...] = coeff_ref[...].astype(F32).reshape(n_atoms * funcs, columns)
    by_atom = jnp.concatenate(
        [coeff_f[pl.ds(m, n_atoms, stride=funcs), :].astype(BF16) for m in range(funcs)], axis=1
    )
    packed = jnp.dot(pick, by_atom, preferred_element_type=F32)
    for s in range(2):
        for m in range(funcs):
            out_f[pl.ds(s * funcs + m, n_clust, stride=2 * funcs), :] = packed[
                s * n_clust : (s + 1) * n_clust, m * columns : (m + 1) * columns
            ]
    out_buf[...] = out_f[...].astype(BF16)

    pl.semaphore_wait(barrier, first_later - 1 + len(TARGETS))

    def a2a(to, source):
        return pltpu.make_async_remote_copy(
            src_ref=out_buf.at[pl.ds(pl.multiple_of(to * 16, 16), 16)],
            dst_ref=in_buf.at[pl.ds(pl.multiple_of(source * 16, 16), 16)],
            send_sem=a2a_send.at[to],
            recv_sem=a2a_recv.at[source],
            device_id=(to, b),
            device_id_type=MESH,
        )

    def a2a_start(to, _):
        @pl.when(to != c)
        def _():
            a2a(to, c).start()

        return 0

    lax.fori_loop(0, first_later, a2a_start, 0)
    begin_basis, relay_basis, relay_basis_last, finish_basis = exchange(
        n_y, basis_hbm, blocks, b_send, b_recv
    )
    begin_basis()
    basis_load.start()
    coul_load.start()

    own_list = inter_ref[pl.ds(c, 1), :]
    own_owner = (own_list // n_atoms).astype(F32)
    entry = lax.broadcasted_iota(jnp.int32, (rows, n_list), 0) // funcs
    column = lax.broadcasted_iota(jnp.int32, (rows, n_list), 1)
    own_row = jnp.broadcast_to(own_owner, (rows, n_list))
    owner_col = jnp.sum(jnp.where(entry == column, own_row, 0.0), axis=1, keepdims=True)
    own_rank = jnp.sum(
        jnp.where((own_row == owner_col) & (column < entry), 1.0, 0.0), axis=1, keepdims=True
    )
    func_col = (lax.broadcasted_iota(jnp.int32, (rows, 1), 0) % funcs).astype(F32)
    place = owner_col * (2 * funcs) + own_rank * funcs + func_col
    unpack = (
        lax.broadcasted_iota(jnp.int32, (rows, slot_rows), 1).astype(F32) == place
    ).astype(BF16)
    own_at = pl.ds(pl.multiple_of(c * 16, 16), 16)
    in_buf[own_at, :] = out_buf[own_at, :]

    def a2a_wait(source, _):
        @pl.when(source != c)
        def _():
            a2a(c, source).wait_recv()

        return 0

    lax.fori_loop(first_mate, first_later, a2a_wait, 0)
    relay_basis()

    def answer(source, _):
        a2a(c, source).wait_recv()
        a2a(source, c).start()
        return 0

    for later in range(1, GROUPS):
        if later == GROUPS // 2:
            pl.when(mine < later)(relay_basis_last)

        @pl.when(mine < later)
        def _():
            lax.fori_loop(later * group, (later + 1) * group, answer, 0)

    pl.when(mine >= GROUPS // 2)(relay_basis_last)
    lax.fori_loop(0, first_mate, a2a_wait, 0)
    chunk = jnp.dot(unpack, in_buf[...], preferred_element_type=F32)
    n_buf[b] = chunk.astype(BF16)

    def chunk_at(plane, dist):
        return at(y + dist, z if plane == 0 else 1 - z, n_y)

    part_rows = rows // PARTS

    def send(k):
        rise, across, plane, dist, first, end = SENDS[k]
        where = n_buf.at[
            chunk_at(plane, dist), pl.ds(first * part_rows, (end - first) * part_rows)
        ]
        return pltpu.make_async_remote_copy(
            src_ref=where,
            dst_ref=where,
            send_sem=ag_send.at[k],
            recv_sem=ag_recv.at[k],
            device_id=(c, at(y + rise, 1 - z if across else z, n_y)),
            device_id_type=MESH,
        )

    have = set()

    def need(plane, dist, first=0, end=PARTS):
        if (plane, dist) == (0, 0):
            return
        for part in range(first, end):
            k = CAME[(plane, wrapped(dist), part)]
            if k not in have:
                have.add(k)
                send(k).wait_recv()

    for k in range(len(FIRST)):
        send(k).start()
    k = len(FIRST)
    folded = False
    for item in THEN:
        if len(item) == 6:
            need(*item[2:])
            send(k).start()
            k += 1
        else:
            for chunk_of in item:
                need(*chunk_of)
            both = jnp.concatenate([n_buf[chunk_at(*chunk_of)] for chunk_of in item], axis=1)
            term = lax.dot_general(both, both, (((1,), (1,)), ((), ())), preferred_element_type=F32)
            g_ref[...] = g_ref[...] + term if folded else term
            folded = True
    finish_basis()

    basis_load.wait()
    basis = basis_ref[...]
    scale = (n_buf.shape[0] * n_buf.shape[2]) ** -0.5
    g = g_ref[...]
    g_hi = g.astype(BF16)
    g_lo = (g - g_hi.astype(F32)).astype(BF16)
    h = jnp.dot(basis, g_hi, preferred_element_type=F32) + jnp.dot(
        basis, g_lo, preferred_element_type=F32
    )
    h = (h * scale).astype(BF16)
    coul_load.wait()
    reach = reach_ref[0]
    w = None
    for slot_at, offset in [(None, 0)] + list(SLOT_OFFSET.items()):
        other = basis if slot_at is None else blocks[slot_at]
        density = lax.dot_general(h, other, (((1,), (1,)), ((), ())), preferred_element_type=F32)
        within = jnp.where(abs(offset) <= reach, F32(1.0), F32(0.0))
        coul = coul_v[half_stops + sign * offset].astype(F32) * within
        tile = (density * coul).astype(BF16)
        term = jnp.dot(tile, other, preferred_element_type=F32)
        w = term if w is None else w + term
    w_out[...] = w.astype(BF16)

    def a2a_sent(to, _):
        @pl.when(to != c)
        def _():
            a2a(to, c).wait_send()

        return 0

    lax.fori_loop(0, n_clust, a2a_sent, 0)
    for k in range(len(SENDS)):
        send(k).wait_send()


def apply_kernel(w_ref, n_ref, out_hbm, out_v, sem):
    w = w_ref[...]
    width = 2 * n_ref.shape[2]
    copies = []
    for j in range(n_ref.shape[0] // 2):
        both = jnp.concatenate([n_ref[2 * j], n_ref[2 * j + 1]], axis=1)
        where = slice(j * width, (j + 1) * width)
        out_v[:, where] = jnp.dot(w, both, preferred_element_type=F32).astype(BF16)
        copy = pltpu.make_async_copy(out_v.at[:, where], out_hbm.at[:, where], sem.at[j])
        copy.start()
        copies.append(copy)
    for copy in copies:
        copy.wait()


def solution(mesh):
    n_clust, n_blk = mesh.shape["cluster"], mesh.shape["blk"]
    n_y = n_blk // 2

    def on_device(coeff, intersection, basis_vals, coulomb, reach):
        rows, funcs = basis_vals.shape
        columns = coeff.shape[2]
        stops = coulomb.shape[1]
        vmem = pl.BlockSpec(memory_space=pltpu.VMEM)
        hbm = pl.BlockSpec(memory_space=pltpu.HBM)

        def stay(x):
            return pltpu.with_memory_space_constraint(x, pltpu.HBM)

        basis_vals = stay(basis_vals)

        def gather(*refs):
            gather_kernel(n_y, n_clust, *refs)

        needed, w = pl.pallas_call(
            gather,
            out_shape=(
                jax.ShapeDtypeStruct((n_blk, funcs, columns), BF16),
                jax.ShapeDtypeStruct((rows, funcs), BF16),
            ),
            in_specs=[hbm, hbm, hbm, hbm, pl.BlockSpec(memory_space=pltpu.SMEM)],
            out_specs=(vmem, vmem),
            scratch_shapes=[
                pltpu.VMEM(coeff.shape, BF16),
                pltpu.VMEM(intersection.shape, jnp.int32),
                pltpu.VMEM((rows, funcs), BF16),
                pltpu.VMEM((stops, rows, rows), BF16),
                pltpu.VMEM((coeff.shape[0] * coeff.shape[1], columns), F32),
                pltpu.VMEM((16 * n_clust, columns), F32),
                pltpu.VMEM((16 * n_clust, columns), BF16),
                pltpu.VMEM((16 * n_clust, columns), BF16),
                pltpu.VMEM((6, rows, funcs), BF16),
                pltpu.VMEM((funcs, funcs), F32),
                pltpu.SemaphoreType.DMA((4,)),
                pltpu.SemaphoreType.DMA((n_clust,)),
                pltpu.SemaphoreType.DMA((n_clust,)),
                pltpu.SemaphoreType.DMA((6,)),
                pltpu.SemaphoreType.DMA((6,)),
                pltpu.SemaphoreType.DMA((len(SENDS),)),
                pltpu.SemaphoreType.DMA((len(SENDS),)),
            ],
            compiler_params=pltpu.CompilerParams(
                collective_id=0, has_side_effects=True, vmem_limit_bytes=32 * 2**20
            ),
            name="gather",
        )(
            stay(coeff),
            stay(intersection),
            basis_vals,
            stay(jnp.swapaxes(coulomb, 0, 1)),
            reach,
        )

        return pl.pallas_call(
            apply_kernel,
            out_shape=jax.ShapeDtypeStruct((rows, n_blk * columns), BF16),
            in_specs=[vmem, vmem],
            out_specs=hbm,
            scratch_shapes=[
                pltpu.VMEM((rows, n_blk * columns), BF16),
                pltpu.SemaphoreType.DMA((n_blk // 2,)),
            ],
            compiler_params=pltpu.CompilerParams(vmem_limit_bytes=16 * 2**20),
            name="apply",
        )(w, needed)

    return jax.shard_map(
        on_device,
        mesh=mesh,
        in_specs=(
            P("cluster", None, "blk"),
            P(),
            P(("cluster", "blk"), None),
            P(("cluster", "blk"), None, None),
            P(("cluster", "blk")),
        ),
        out_specs=P(("cluster", "blk"), None),
        check_vma=False,
    )
```

```python
import jax
import jax.numpy as jnp
from jax import lax
from jax.experimental import pallas as pl
from jax.experimental.pallas import tpu as pltpu
from jax.sharding import PartitionSpec as P

MESH = pl.DeviceIdType.MESH
F32 = jnp.float32
BF16 = jnp.bfloat16

PART, UP, DOWN, PART_UP, PART_DOWN, PART_DOWN2 = range(6)
SLOT_OFFSET = {PART: 1, UP: 2, DOWN: -2, PART_UP: 3, PART_DOWN: -1, PART_DOWN2: -3}

GROUPS = 4
PIECES = 4
PARTS = 4
FIRST = [
    (-1, 0, 0, 0, 0, 2),
    (1, 0, 0, 0, 0, 2),
    (0, 1, 0, 0, 2, 4),
    (-2, 0, 0, 0, 2, 4),
    (2, 0, 0, 0, 2, 4),
    (0, 1, 0, 0, 0, 2),
    (-1, 0, 0, 0, 2, 4),
    (1, 0, 0, 0, 2, 4),
]
THEN = [
    (0, 1, 0, 1, 0, 2),
    (0, 1, 0, -1, 0, 2),
    (-2, 0, 0, 1, 0, 2),
    (2, 0, 0, -1, 0, 2),
    (0, 1, 0, 2, 2, 4),
    (0, 1, 0, -2, 2, 4),
    (-1, 0, 0, 2, 2, 4),
    (1, 0, 0, -2, 2, 4),
    (-1, 0, 0, 1, 0, 2),
    (1, 0, 0, -1, 0, 2),
    (-1, 0, 1, 0, 2, 4),
    (1, 0, 1, 0, 2, 4),
    (-1, 0, 1, 1, 0, 2),
    (1, 0, 1, -1, 0, 2),
    (0, 1, 0, 3, 0, 2),
    (0, 1, 0, -3, 0, 2),
    (1, 1, 0, -3, 0, 2),
    (-1, 1, 0, 3, 2, 4),
    (-1, 0, 0, 3, 0, 2),
    (1, 0, 0, -3, 2, 4),
    (-1, 0, 1, 2, 2, 4),
    (1, 0, 1, -2, 2, 4),
    ((0, 0), (1, 0)),
    ((0, 1), (0, -1)),
    ((0, 3), (0, -3)),
    ((0, 2), (0, -2)),
    ((1, 1), (1, -1)),
    ((1, 2), (1, -2)),
    ((0, 4), (1, -3)),
    ((1, 4), (1, 3)),
]
TARGETS = sorted(
    {s[:2] for s in FIRST} | {s[:2] for s in THEN if len(s) == 6},
    key=lambda t: (-abs(t[0]) - t[1], t),
)
SENDS = FIRST + [s for s in THEN if len(s) == 6]


def wrapped(dist):
    return (dist + 3) % 8 - 3


def arrivals():
    came = {}
    for k, (up, across, plane, dist, first, end) in enumerate(SENDS):
        for part in range(first, end):
            key = ((plane + across) % 2, wrapped(dist - up), part)
            assert key not in came and key[:2] != (0, 0)
            came[key] = k
    assert len(came) == 15 * PARTS
    return came


CAME = arrivals()


def at(yy, zz, n_y):
    return lax.rem(yy + 2 * n_y, n_y) * 2 + zz


def exchange(n_y, basis_hbm, blocks, send_sem, recv_sem):
    c = lax.axis_index("cluster")
    b = lax.axis_index("blk")
    y, z = b // 2, b % 2
    sign = 1 - 2 * z
    up, down, across = at(y + sign, z, n_y), at(y - sign, z, n_y), at(y, 1 - z, n_y)

    part = basis_hbm.shape[0] // PIECES

    def copy(src, slot_at, to):
        made = []
        for k in range(PIECES):
            some = pl.ds(k * part, part)
            made.append(
                pltpu.make_async_remote_copy(
                    src_ref=basis_hbm.at[some] if src is None else blocks.at[src, some],
                    dst_ref=blocks.at[slot_at, some],
                    send_sem=send_sem.at[slot_at, k],
                    recv_sem=recv_sem.at[slot_at, k],
                    device_id=(c, to),
                    device_id_type=MESH,
                )
            )
        return made

    copies = [
        copy(None, PART, across),
        copy(None, UP, down),
        copy(None, DOWN, up),
        copy(PART, PART_UP, down),
        copy(UP, PART_DOWN, across),
        copy(PART_DOWN, PART_DOWN2, up),
    ]

    def begin():
        for k in range(PIECES):
            for slot_at in (PART, UP, DOWN):
                copies[slot_at][k].start()

    def relay():
        for k in range(PIECES):
            copies[PART][k].wait_recv()
            copies[PART_UP][k].start()
            copies[UP][k].wait_recv()
            copies[PART_DOWN][k].start()

    def relay_last():
        for k in range(PIECES):
            copies[PART_DOWN][k].wait_recv()
            copies[PART_DOWN2][k].start()

    def finish():
        for k in range(PIECES):
            for slot_at in (DOWN, PART_UP, PART_DOWN2):
                copies[slot_at][k].wait_recv()
        for k in range(PIECES):
            for slot_at in range(6):
                copies[slot_at][k].wait_send()

    return begin, relay, relay_last, finish


def gather_kernel(
    n_y, n_clust, coeff_hbm, inter_hbm, basis_hbm, coul_hbm, reach_ref,
    n_buf, w_out,
    coeff_ref, inter_ref, basis_ref, coul_v, coeff_f, out_f, out_buf, in_buf, blocks, g_ref,
    load_sem, a2a_send, a2a_recv, b_send, b_recv, ag_send, ag_recv,
):
    c = lax.axis_index("cluster")
    b = lax.axis_index("blk")
    y, z = b // 2, b % 2
    sign = 1 - 2 * z
    rows = basis_ref.shape[0]
    stops = coul_v.shape[0]
    half_stops = (stops - 1) // 2

    inter_load, coeff_load, basis_load, coul_load = [
        pltpu.make_async_copy(src, dst, load_sem.at[k])
        for k, (src, dst) in enumerate(
            (
                (inter_hbm, inter_ref),
                (coeff_hbm, coeff_ref),
                (basis_hbm, basis_ref),
                (coul_hbm, coul_v),
            )
        )
    ]
    inter_load.start()
    coeff_load.start()

    barrier = pltpu.get_barrier_semaphore()

    group = n_clust // GROUPS
    mine = c // group
    first_mate, first_later = mine * group, (mine + 1) * group

    def greet(to, _):
        @pl.when(to != c)
        def _():
            pl.semaphore_signal(barrier, inc=1, device_id=(to, b), device_id_type=MESH)

        return 0

    def greet_row(rise, across):
        pl.semaphore_signal(
            barrier,
            inc=1,
            device_id=(c, at(y + rise, 1 - z if across else z, n_y)),
            device_id_type=MESH,
        )

    for target in TARGETS:
        if abs(target[0]) + target[1] >= 2:
            greet_row(*target)
    lax.fori_loop(first_mate, n_clust, greet, 0)
    for target in TARGETS:
        if abs(target[0]) + target[1] < 2:
            greet_row(*target)

    inter_load.wait()
    inter = inter_ref[...]
    n_list = inter.shape[1]
    n_atoms, funcs, columns = coeff_ref.shape
    slot_rows = 2 * funcs * n_clust
    owner = inter // n_atoms
    key = lax.broadcasted_iota(jnp.int32, inter.shape, 1) * n_atoms + (inter - owner * n_atoms)
    key = key.astype(F32)
    top = F32(n_list * n_atoms)
    low = jnp.min(jnp.where(owner == c, key, top), axis=1, keepdims=True)
    high = jnp.max(jnp.where(owner == c, key, -1.0), axis=1, keepdims=True)
    low_at = jnp.where(low < top, low.astype(jnp.int32) % n_atoms, -1)
    high_at = jnp.where(high > low, high.astype(jnp.int32) % n_atoms, -1)
    atom = lax.broadcasted_iota(jnp.int32, (n_clust, n_atoms), 1)
    pick = jnp.concatenate([atom == low_at, atom == high_at], axis=0).astype(F32).astype(BF16)
    coeff_load.wait()
    coeff_f[...] = coeff_ref[...].astype(F32).reshape(n_atoms * funcs, columns)
    by_atom = jnp.concatenate(
        [coeff_f[pl.ds(m, n_atoms, stride=funcs), :].astype(BF16) for m in range(funcs)], axis=1
    )
    packed = jnp.dot(pick, by_atom, preferred_element_type=F32)
    for s in range(2):
        for m in range(funcs):
            out_f[pl.ds(s * funcs + m, n_clust, stride=2 * funcs), :] = packed[
                s * n_clust : (s + 1) * n_clust, m * columns : (m + 1) * columns
            ]
    out_buf[...] = out_f[...].astype(BF16)

    pl.semaphore_wait(barrier, first_later - 1 + len(TARGETS))

    def a2a(to, source):
        return pltpu.make_async_remote_copy(
            src_ref=out_buf.at[pl.ds(pl.multiple_of(to * 16, 16), 16)],
            dst_ref=in_buf.at[pl.ds(pl.multiple_of(source * 16, 16), 16)],
            send_sem=a2a_send.at[to],
            recv_sem=a2a_recv.at[source],
            device_id=(to, b),
            device_id_type=MESH,
        )

    def a2a_start(to, _):
        @pl.when(to != c)
        def _():
            a2a(to, c).start()

        return 0

    lax.fori_loop(0, first_later, a2a_start, 0)
    begin_basis, relay_basis, relay_basis_last, finish_basis = exchange(
        n_y, basis_hbm, blocks, b_send, b_recv
    )
    begin_basis()
    basis_load.start()
    coul_load.start()

    own_list = inter_ref[pl.ds(c, 1), :]
    own_owner = (own_list // n_atoms).astype(F32)
    entry = lax.broadcasted_iota(jnp.int32, (rows, n_list), 0) // funcs
    column = lax.broadcasted_iota(jnp.int32, (rows, n_list), 1)
    own_row = jnp.broadcast_to(own_owner, (rows, n_list))
    owner_col = jnp.sum(jnp.where(entry == column, own_row, 0.0), axis=1, keepdims=True)
    own_rank = jnp.sum(
        jnp.where((own_row == owner_col) & (column < entry), 1.0, 0.0), axis=1, keepdims=True
    )
    func_col = (lax.broadcasted_iota(jnp.int32, (rows, 1), 0) % funcs).astype(F32)
    place = owner_col * (2 * funcs) + own_rank * funcs + func_col
    unpack = (
        lax.broadcasted_iota(jnp.int32, (rows, slot_rows), 1).astype(F32) == place
    ).astype(BF16)
    own_at = pl.ds(pl.multiple_of(c * 16, 16), 16)
    in_buf[own_at, :] = out_buf[own_at, :]

    def a2a_wait(source, _):
        @pl.when(source != c)
        def _():
            a2a(c, source).wait_recv()

        return 0

    lax.fori_loop(first_mate, first_later, a2a_wait, 0)
    relay_basis()

    def answer(source, _):
        a2a(c, source).wait_recv()
        a2a(source, c).start()
        return 0

    for later in range(1, GROUPS):
        if later == GROUPS // 2:
            pl.when(mine < later)(relay_basis_last)

        @pl.when(mine < later)
        def _():
            lax.fori_loop(later * group, (later + 1) * group, answer, 0)

    pl.when(mine >= GROUPS // 2)(relay_basis_last)
    lax.fori_loop(0, first_mate, a2a_wait, 0)
    chunk = jnp.dot(unpack, in_buf[...], preferred_element_type=F32)
    n_buf[b] = chunk.astype(BF16)

    def chunk_at(plane, dist):
        return at(y + dist, z if plane == 0 else 1 - z, n_y)

    part_rows = rows // PARTS

    def send(k):
        rise, across, plane, dist, first, end = SENDS[k]
        where = n_buf.at[
            chunk_at(plane, dist), pl.ds(first * part_rows, (end - first) * part_rows)
        ]
        return pltpu.make_async_remote_copy(
            src_ref=where,
            dst_ref=where,
            send_sem=ag_send.at[k],
            recv_sem=ag_recv.at[k],
            device_id=(c, at(y + rise, 1 - z if across else z, n_y)),
            device_id_type=MESH,
        )

    have = set()

    def need(plane, dist, first=0, end=PARTS):
        if (plane, dist) == (0, 0):
            return
        for part in range(first, end):
            k = CAME[(plane, wrapped(dist), part)]
            if k not in have:
                have.add(k)
                send(k).wait_recv()

    for k in range(len(FIRST)):
        send(k).start()
    k = len(FIRST)
    folded = False
    for item in THEN:
        if len(item) == 6:
            need(*item[2:])
            send(k).start()
            k += 1
        else:
            for chunk_of in item:
                need(*chunk_of)
            both = jnp.concatenate([n_buf[chunk_at(*chunk_of)] for chunk_of in item], axis=1)
            term = lax.dot_general(both, both, (((1,), (1,)), ((), ())), preferred_element_type=F32)
            g_ref[...] = g_ref[...] + term if folded else term
            folded = True
    finish_basis()

    basis_load.wait()
    basis = basis_ref[...]
    scale = (n_buf.shape[0] * n_buf.shape[2]) ** -0.5
    g = g_ref[...]
    g_hi = g.astype(BF16)
    g_lo = (g - g_hi.astype(F32)).astype(BF16)
    h = jnp.dot(basis, g_hi, preferred_element_type=F32) + jnp.dot(
        basis, g_lo, preferred_element_type=F32
    )
    h = (h * scale).astype(BF16)
    coul_load.wait()
    reach = reach_ref[0]
    w = None
    for slot_at, offset in [(None, 0)] + list(SLOT_OFFSET.items()):
        other = basis if slot_at is None else blocks[slot_at]
        density = lax.dot_general(h, other, (((1,), (1,)), ((), ())), preferred_element_type=F32)
        within = jnp.where(abs(offset) <= reach, F32(1.0), F32(0.0))
        coul = coul_v[half_stops + sign * offset].astype(F32) * within
        tile = (density * coul).astype(BF16)
        term = jnp.dot(tile, other, preferred_element_type=F32)
        w = term if w is None else w + term
    w_out[...] = w.astype(BF16)

    def a2a_sent(to, _):
        @pl.when(to != c)
        def _():
            a2a(to, c).wait_send()

        return 0

    lax.fori_loop(0, n_clust, a2a_sent, 0)
    for k in range(len(SENDS)):
        send(k).wait_send()


def apply_kernel(w_ref, n_ref, out_hbm, out_v, sem):
    w = w_ref[...]
    width = 2 * n_ref.shape[2]
    copies = []
    for j in range(n_ref.shape[0] // 2):
        both = jnp.concatenate([n_ref[2 * j], n_ref[2 * j + 1]], axis=1)
        where = slice(j * width, (j + 1) * width)
        out_v[:, where] = jnp.dot(w, both, preferred_element_type=F32).astype(BF16)
        copy = pltpu.make_async_copy(out_v.at[:, where], out_hbm.at[:, where], sem.at[j])
        copy.start()
        copies.append(copy)
    for copy in copies:
        copy.wait()


def solution(mesh):
    n_clust, n_blk = mesh.shape["cluster"], mesh.shape["blk"]
    n_y = n_blk // 2

    def on_device(coeff, intersection, basis_vals, coulomb, reach):
        rows, funcs = basis_vals.shape
        columns = coeff.shape[2]
        stops = coulomb.shape[1]
        vmem = pl.BlockSpec(memory_space=pltpu.VMEM)
        hbm = pl.BlockSpec(memory_space=pltpu.HBM)

        def stay(x):
            return pltpu.with_memory_space_constraint(x, pltpu.HBM)

        basis_vals = stay(basis_vals)

        def gather(*refs):
            gather_kernel(n_y, n_clust, *refs)

        needed, w = pl.pallas_call(
            gather,
            out_shape=(
                jax.ShapeDtypeStruct((n_blk, funcs, columns), BF16),
                jax.ShapeDtypeStruct((rows, funcs), BF16),
            ),
            in_specs=[hbm, hbm, hbm, hbm, pl.BlockSpec(memory_space=pltpu.SMEM)],
            out_specs=(vmem, vmem),
            scratch_shapes=[
                pltpu.VMEM(coeff.shape, BF16),
                pltpu.VMEM(intersection.shape, jnp.int32),
                pltpu.VMEM((rows, funcs), BF16),
                pltpu.VMEM((stops, rows, rows), BF16),
                pltpu.VMEM((coeff.shape[0] * coeff.shape[1], columns), F32),
                pltpu.VMEM((16 * n_clust, columns), F32),
                pltpu.VMEM((16 * n_clust, columns), BF16),
                pltpu.VMEM((16 * n_clust, columns), BF16),
                pltpu.VMEM((6, rows, funcs), BF16),
                pltpu.VMEM((funcs, funcs), F32),
                pltpu.SemaphoreType.DMA((4,)),
                pltpu.SemaphoreType.DMA((n_clust,)),
                pltpu.SemaphoreType.DMA((n_clust,)),
                pltpu.SemaphoreType.DMA((6, PIECES)),
                pltpu.SemaphoreType.DMA((6, PIECES)),
                pltpu.SemaphoreType.DMA((len(SENDS),)),
                pltpu.SemaphoreType.DMA((len(SENDS),)),
            ],
            compiler_params=pltpu.CompilerParams(
                collective_id=0, has_side_effects=True, vmem_limit_bytes=32 * 2**20
            ),
            name="gather",
        )(
            stay(coeff),
            stay(intersection),
            basis_vals,
            stay(jnp.swapaxes(coulomb, 0, 1)),
            reach,
        )

        return pl.pallas_call(
            apply_kernel,
            out_shape=jax.ShapeDtypeStruct((rows, n_blk * columns), BF16),
            in_specs=[vmem, vmem],
            out_specs=hbm,
            scratch_shapes=[
                pltpu.VMEM((rows, n_blk * columns), BF16),
                pltpu.SemaphoreType.DMA((n_blk // 2,)),
            ],
            compiler_params=pltpu.CompilerParams(vmem_limit_bytes=16 * 2**20),
            name="apply",
        )(w, needed)

    return jax.shard_map(
        on_device,
        mesh=mesh,
        in_specs=(
            P("cluster", None, "blk"),
            P(),
            P(("cluster", "blk"), None),
            P(("cluster", "blk"), None, None),
            P(("cluster", "blk")),
        ),
        out_specs=P(("cluster", "blk"), None),
        check_vma=False,
    )
```

```python
import jax
import jax.numpy as jnp
from jax import lax
from jax.experimental import pallas as pl
from jax.experimental.pallas import tpu as pltpu
from jax.sharding import PartitionSpec as P

MESH = pl.DeviceIdType.MESH
F32 = jnp.float32
BF16 = jnp.bfloat16

PART, UP, DOWN, PART_UP, PART_DOWN, PART_DOWN2 = range(6)
SLOT_OFFSET = {PART: 1, UP: 2, DOWN: -2, PART_UP: 3, PART_DOWN: -1, PART_DOWN2: -3}

GROUPS = 4
PIECES = 4
LAST_SENDS = 8
PARTS = 4
FIRST = [
    (-1, 0, 0, 0, 0, 2),
    (1, 0, 0, 0, 0, 2),
    (0, 1, 0, 0, 2, 4),
    (-2, 0, 0, 0, 2, 4),
    (2, 0, 0, 0, 2, 4),
    (0, 1, 0, 0, 0, 2),
    (-1, 0, 0, 0, 2, 4),
    (1, 0, 0, 0, 2, 4),
]
THEN = [
    (0, 1, 0, 1, 0, 2),
    (0, 1, 0, -1, 0, 2),
    (-2, 0, 0, 1, 0, 2),
    (2, 0, 0, -1, 0, 2),
    (0, 1, 0, 2, 2, 4),
    (0, 1, 0, -2, 2, 4),
    (-1, 0, 0, 2, 2, 4),
    (1, 0, 0, -2, 2, 4),
    (-1, 0, 0, 1, 0, 2),
    (1, 0, 0, -1, 0, 2),
    (-1, 0, 1, 0, 2, 4),
    (1, 0, 1, 0, 2, 4),
    (-1, 0, 1, 1, 0, 2),
    (1, 0, 1, -1, 0, 2),
    (0, 1, 0, 3, 0, 2),
    (0, 1, 0, -3, 0, 2),
    (1, 1, 0, -3, 0, 2),
    (-1, 1, 0, 3, 2, 4),
    (-1, 0, 0, 3, 0, 2),
    (1, 0, 0, -3, 2, 4),
    (-1, 0, 1, 2, 2, 4),
    (1, 0, 1, -2, 2, 4),
    ((0, 0), (1, 0)),
    ((0, 1), (0, -1)),
    ((0, 3), (0, -3)),
    ((0, 2), (0, -2)),
    ((1, 1), (1, -1)),
    ((1, 2), (1, -2)),
    ((0, 4), (1, -3)),
    ((1, 4), (1, 3)),
]
TARGETS = sorted(
    {s[:2] for s in FIRST} | {s[:2] for s in THEN if len(s) == 6},
    key=lambda t: (-abs(t[0]) - t[1], t),
)
SENDS = FIRST + [s for s in THEN if len(s) == 6]


def wrapped(dist):
    return (dist + 3) % 8 - 3


def arrivals():
    came = {}
    for k, (up, across, plane, dist, first, end) in enumerate(SENDS):
        for part in range(first, end):
            key = ((plane + across) % 2, wrapped(dist - up), part)
            assert key not in came and key[:2] != (0, 0)
            came[key] = k
    assert len(came) == 15 * PARTS
    return came


CAME = arrivals()


def at(yy, zz, n_y):
    return lax.rem(yy + 2 * n_y, n_y) * 2 + zz


def exchange(n_y, basis_hbm, blocks, send_sem, recv_sem):
    c = lax.axis_index("cluster")
    b = lax.axis_index("blk")
    y, z = b // 2, b % 2
    sign = 1 - 2 * z
    up, down, across = at(y + sign, z, n_y), at(y - sign, z, n_y), at(y, 1 - z, n_y)

    part = basis_hbm.shape[0] // PIECES

    def copy(src, slot_at, to):
        made = []
        for k in range(PIECES):
            some = pl.ds(k * part, part)
            made.append(
                pltpu.make_async_remote_copy(
                    src_ref=basis_hbm.at[some] if src is None else blocks.at[src, some],
                    dst_ref=blocks.at[slot_at, some],
                    send_sem=send_sem.at[slot_at, k],
                    recv_sem=recv_sem.at[slot_at, k],
                    device_id=(c, to),
                    device_id_type=MESH,
                )
            )
        return made

    copies = [
        copy(None, PART, across),
        copy(None, UP, down),
        copy(None, DOWN, up),
        copy(PART, PART_UP, down),
        copy(UP, PART_DOWN, across),
        copy(PART_DOWN, PART_DOWN2, up),
    ]

    def begin():
        for k in range(PIECES):
            for slot_at in (PART, UP, DOWN):
                copies[slot_at][k].start()

    def relay():
        for k in range(PIECES):
            copies[PART][k].wait_recv()
            copies[PART_UP][k].start()
            copies[UP][k].wait_recv()
            copies[PART_DOWN][k].start()

    def relay_last():
        for k in range(PIECES):
            copies[PART_DOWN][k].wait_recv()
            copies[PART_DOWN2][k].start()

    def finish():
        for k in range(PIECES):
            for slot_at in (DOWN, PART_UP, PART_DOWN2):
                copies[slot_at][k].wait_recv()
        for k in range(PIECES):
            for slot_at in range(6):
                copies[slot_at][k].wait_send()

    return begin, relay, relay_last, finish


def gather_kernel(
    n_y, n_clust, coeff_hbm, inter_hbm, basis_hbm, coul_hbm, reach_ref,
    n_buf, w_out,
    coeff_ref, inter_ref, basis_ref, coul_v, coeff_f, out_f, out_buf, in_buf, blocks, g_ref,
    load_sem, a2a_send, a2a_recv, b_send, b_recv, ag_send, ag_recv,
):
    c = lax.axis_index("cluster")
    b = lax.axis_index("blk")
    y, z = b // 2, b % 2
    sign = 1 - 2 * z
    rows = basis_ref.shape[0]
    stops = coul_v.shape[0]
    half_stops = (stops - 1) // 2

    inter_load, coeff_load, basis_load, coul_load = [
        pltpu.make_async_copy(src, dst, load_sem.at[k])
        for k, (src, dst) in enumerate(
            (
                (inter_hbm, inter_ref),
                (coeff_hbm, coeff_ref),
                (basis_hbm, basis_ref),
                (coul_hbm, coul_v),
            )
        )
    ]
    inter_load.start()
    coeff_load.start()

    barrier = pltpu.get_barrier_semaphore()

    group = n_clust // GROUPS
    mine = c // group
    first_mate, first_later = mine * group, (mine + 1) * group

    def greet(to, _):
        pl.semaphore_signal(barrier, inc=1, device_id=(to, b), device_id_type=MESH)
        return 0

    def greet_row(rise, across):
        pl.semaphore_signal(
            barrier,
            inc=1,
            device_id=(c, at(y + rise, 1 - z if across else z, n_y)),
            device_id_type=MESH,
        )

    def greet_mate(step):
        to = first_mate + (c - first_mate + step) % group
        pl.semaphore_signal(barrier, inc=1, device_id=(to, b), device_id_type=MESH)

    middle = sorted(range(1, group), key=lambda step: (abs(step - group // 2), step))
    for step in middle[:3]:
        greet_mate(step)
    for target in TARGETS:
        if abs(target[0]) + target[1] >= 2:
            greet_row(*target)
    for step in middle[3:]:
        greet_mate(step)
    for target in TARGETS:
        if abs(target[0]) + target[1] < 2:
            greet_row(*target)
    lax.fori_loop(first_later, n_clust, greet, 0)

    inter_load.wait()
    inter = inter_ref[...]
    n_list = inter.shape[1]
    n_atoms, funcs, columns = coeff_ref.shape
    slot_rows = 2 * funcs * n_clust
    owner = inter // n_atoms
    key = lax.broadcasted_iota(jnp.int32, inter.shape, 1) * n_atoms + (inter - owner * n_atoms)
    key = key.astype(F32)
    top = F32(n_list * n_atoms)
    low = jnp.min(jnp.where(owner == c, key, top), axis=1, keepdims=True)
    high = jnp.max(jnp.where(owner == c, key, -1.0), axis=1, keepdims=True)
    low_at = jnp.where(low < top, low.astype(jnp.int32) % n_atoms, -1)
    high_at = jnp.where(high > low, high.astype(jnp.int32) % n_atoms, -1)
    atom = lax.broadcasted_iota(jnp.int32, (n_clust, n_atoms), 1)
    pick = jnp.concatenate([atom == low_at, atom == high_at], axis=0).astype(F32).astype(BF16)
    coeff_load.wait()
    coeff_f[...] = coeff_ref[...].astype(F32).reshape(n_atoms * funcs, columns)
    by_atom = jnp.concatenate(
        [coeff_f[pl.ds(m, n_atoms, stride=funcs), :].astype(BF16) for m in range(funcs)], axis=1
    )
    packed = jnp.dot(pick, by_atom, preferred_element_type=F32)
    for s in range(2):
        for m in range(funcs):
            out_f[pl.ds(s * funcs + m, n_clust, stride=2 * funcs), :] = packed[
                s * n_clust : (s + 1) * n_clust, m * columns : (m + 1) * columns
            ]
    out_buf[...] = out_f[...].astype(BF16)

    pl.semaphore_wait(barrier, first_later - 1 + len(TARGETS))

    def a2a(to, source):
        return pltpu.make_async_remote_copy(
            src_ref=out_buf.at[pl.ds(pl.multiple_of(to * 16, 16), 16)],
            dst_ref=in_buf.at[pl.ds(pl.multiple_of(source * 16, 16), 16)],
            send_sem=a2a_send.at[to],
            recv_sem=a2a_recv.at[source],
            device_id=(to, b),
            device_id_type=MESH,
        )

    def a2a_start(to, _):
        @pl.when(to != c)
        def _():
            a2a(to, c).start()

        return 0

    lax.fori_loop(0, first_later, a2a_start, 0)
    begin_basis, relay_basis, relay_basis_last, finish_basis = exchange(
        n_y, basis_hbm, blocks, b_send, b_recv
    )
    begin_basis()
    basis_load.start()
    coul_load.start()

    own_list = inter_ref[pl.ds(c, 1), :]
    own_owner = (own_list // n_atoms).astype(F32)
    entry = lax.broadcasted_iota(jnp.int32, (rows, n_list), 0) // funcs
    column = lax.broadcasted_iota(jnp.int32, (rows, n_list), 1)
    own_row = jnp.broadcast_to(own_owner, (rows, n_list))
    owner_col = jnp.sum(jnp.where(entry == column, own_row, 0.0), axis=1, keepdims=True)
    own_rank = jnp.sum(
        jnp.where((own_row == owner_col) & (column < entry), 1.0, 0.0), axis=1, keepdims=True
    )
    func_col = (lax.broadcasted_iota(jnp.int32, (rows, 1), 0) % funcs).astype(F32)
    place = owner_col * (2 * funcs) + own_rank * funcs + func_col
    unpack = (
        lax.broadcasted_iota(jnp.int32, (rows, slot_rows), 1).astype(F32) == place
    ).astype(BF16)
    own_at = pl.ds(pl.multiple_of(c * 16, 16), 16)
    in_buf[own_at, :] = out_buf[own_at, :]

    def a2a_wait(source, _):
        @pl.when(source != c)
        def _():
            a2a(c, source).wait_recv()

        return 0

    lax.fori_loop(first_mate, first_later, a2a_wait, 0)
    relay_basis()

    def answer(source, _):
        a2a(c, source).wait_recv()
        a2a(source, c).start()
        return 0

    for later in range(1, GROUPS):
        if later == GROUPS // 2:
            pl.when(mine < later)(relay_basis_last)

        @pl.when(mine < later)
        def _():
            lax.fori_loop(later * group, (later + 1) * group, answer, 0)

    pl.when(mine >= GROUPS // 2)(relay_basis_last)
    lax.fori_loop(0, first_mate, a2a_wait, 0)
    chunk = jnp.dot(unpack, in_buf[...], preferred_element_type=F32)
    n_buf[b] = chunk.astype(BF16)

    def chunk_at(plane, dist):
        return at(y + dist, z if plane == 0 else 1 - z, n_y)

    part_rows = rows // PARTS

    def send(k):
        rise, across, plane, dist, first, end = SENDS[k]
        where = n_buf.at[
            chunk_at(plane, dist), pl.ds(first * part_rows, (end - first) * part_rows)
        ]
        return pltpu.make_async_remote_copy(
            src_ref=where,
            dst_ref=where,
            send_sem=ag_send.at[k],
            recv_sem=ag_recv.at[k],
            device_id=(c, at(y + rise, 1 - z if across else z, n_y)),
            device_id_type=MESH,
        )

    have = set()

    def need(plane, dist, first=0, end=PARTS):
        if (plane, dist) == (0, 0):
            return
        for part in range(first, end):
            k = CAME[(plane, wrapped(dist), part)]
            if k not in have:
                have.add(k)
                send(k).wait_recv()

    for k in range(len(FIRST)):
        send(k).start()
    k = len(FIRST)
    folded = False

    def a2a_sent(to, _):
        @pl.when(to != c)
        def _():
            a2a(to, c).wait_send()

        return 0

    for item in THEN:
        if item == THEN[-2]:
            finish_basis()
            lax.fori_loop(0, n_clust, a2a_sent, 0)
            for j in range(len(SENDS) - LAST_SENDS):
                send(j).wait_send()
        if len(item) == 6:
            need(*item[2:])
            send(k).start()
            k += 1
        else:
            for chunk_of in item:
                need(*chunk_of)
            both = jnp.concatenate([n_buf[chunk_at(*chunk_of)] for chunk_of in item], axis=1)
            term = lax.dot_general(both, both, (((1,), (1,)), ((), ())), preferred_element_type=F32)
            g_ref[...] = g_ref[...] + term if folded else term
            folded = True

    basis_load.wait()
    basis = basis_ref[...]
    scale = (n_buf.shape[0] * n_buf.shape[2]) ** -0.5
    g = g_ref[...]
    g_hi = g.astype(BF16)
    g_lo = (g - g_hi.astype(F32)).astype(BF16)
    h = jnp.dot(basis, g_hi, preferred_element_type=F32) + jnp.dot(
        basis, g_lo, preferred_element_type=F32
    )
    h = (h * scale).astype(BF16)
    coul_load.wait()
    reach = reach_ref[0]
    w = None
    for slot_at, offset in [(None, 0)] + list(SLOT_OFFSET.items()):
        other = basis if slot_at is None else blocks[slot_at]
        density = lax.dot_general(h, other, (((1,), (1,)), ((), ())), preferred_element_type=F32)
        within = jnp.where(abs(offset) <= reach, F32(1.0), F32(0.0))
        coul = coul_v[half_stops + sign * offset].astype(F32) * within
        tile = (density * coul).astype(BF16)
        term = jnp.dot(tile, other, preferred_element_type=F32)
        w = term if w is None else w + term
    w_out[...] = w.astype(BF16)

    for k in range(len(SENDS) - LAST_SENDS, len(SENDS)):
        send(k).wait_send()


def apply_kernel(w_ref, n_ref, out_hbm, out_v, sem):
    w = w_ref[...]
    width = 2 * n_ref.shape[2]
    copies = []
    for j in range(n_ref.shape[0] // 2):
        both = jnp.concatenate([n_ref[2 * j], n_ref[2 * j + 1]], axis=1)
        where = slice(j * width, (j + 1) * width)
        out_v[:, where] = jnp.dot(w, both, preferred_element_type=F32).astype(BF16)
        copy = pltpu.make_async_copy(out_v.at[:, where], out_hbm.at[:, where], sem.at[j])
        copy.start()
        copies.append(copy)
    for copy in copies:
        copy.wait()


def solution(mesh):
    n_clust, n_blk = mesh.shape["cluster"], mesh.shape["blk"]
    n_y = n_blk // 2

    def on_device(coeff, intersection, basis_vals, coulomb, reach):
        rows, funcs = basis_vals.shape
        columns = coeff.shape[2]
        stops = coulomb.shape[1]
        vmem = pl.BlockSpec(memory_space=pltpu.VMEM)
        hbm = pl.BlockSpec(memory_space=pltpu.HBM)

        def stay(x):
            return pltpu.with_memory_space_constraint(x, pltpu.HBM)

        basis_vals = stay(basis_vals)

        def gather(*refs):
            gather_kernel(n_y, n_clust, *refs)

        needed, w = pl.pallas_call(
            gather,
            out_shape=(
                jax.ShapeDtypeStruct((n_blk, funcs, columns), BF16),
                jax.ShapeDtypeStruct((rows, funcs), BF16),
            ),
            in_specs=[hbm, hbm, hbm, hbm, pl.BlockSpec(memory_space=pltpu.SMEM)],
            out_specs=(vmem, vmem),
            scratch_shapes=[
                pltpu.VMEM(coeff.shape, BF16),
                pltpu.VMEM(intersection.shape, jnp.int32),
                pltpu.VMEM((rows, funcs), BF16),
                pltpu.VMEM((stops, rows, rows), BF16),
                pltpu.VMEM((coeff.shape[0] * coeff.shape[1], columns), F32),
                pltpu.VMEM((16 * n_clust, columns), F32),
                pltpu.VMEM((16 * n_clust, columns), BF16),
                pltpu.VMEM((16 * n_clust, columns), BF16),
                pltpu.VMEM((6, rows, funcs), BF16),
                pltpu.VMEM((funcs, funcs), F32),
                pltpu.SemaphoreType.DMA((4,)),
                pltpu.SemaphoreType.DMA((n_clust,)),
                pltpu.SemaphoreType.DMA((n_clust,)),
                pltpu.SemaphoreType.DMA((6, PIECES)),
                pltpu.SemaphoreType.DMA((6, PIECES)),
                pltpu.SemaphoreType.DMA((len(SENDS),)),
                pltpu.SemaphoreType.DMA((len(SENDS),)),
            ],
            compiler_params=pltpu.CompilerParams(
                collective_id=0, has_side_effects=True, vmem_limit_bytes=32 * 2**20
            ),
            name="gather",
        )(
            stay(coeff),
            stay(intersection),
            basis_vals,
            stay(jnp.swapaxes(coulomb, 0, 1)),
            reach,
        )

        return pl.pallas_call(
            apply_kernel,
            out_shape=jax.ShapeDtypeStruct((rows, n_blk * columns), BF16),
            in_specs=[vmem, vmem],
            out_specs=hbm,
            scratch_shapes=[
                pltpu.VMEM((rows, n_blk * columns), BF16),
                pltpu.SemaphoreType.DMA((n_blk // 2,)),
            ],
            compiler_params=pltpu.CompilerParams(vmem_limit_bytes=16 * 2**20),
            name="apply",
        )(w, needed)

    return jax.shard_map(
        on_device,
        mesh=mesh,
        in_specs=(
            P("cluster", None, "blk"),
            P(),
            P(("cluster", "blk"), None),
            P(("cluster", "blk"), None, None),
            P(("cluster", "blk")),
        ),
        out_specs=P(("cluster", "blk"), None),
        check_vma=False,
    )
```

```python
import jax
import jax.numpy as jnp
from jax import lax
from jax.experimental import pallas as pl
from jax.experimental.pallas import tpu as pltpu
from jax.sharding import PartitionSpec as P

MESH = pl.DeviceIdType.MESH
F32 = jnp.float32
BF16 = jnp.bfloat16

PART, UP, DOWN, PART_UP, PART_DOWN, PART_DOWN2 = range(6)
SLOT_OFFSET = {PART: 1, UP: 2, DOWN: -2, PART_UP: 3, PART_DOWN: -1, PART_DOWN2: -3}

GROUPS = 4
PIECES = 4
LAST_SENDS = 8
PARTS = 4
FIRST = [
    (-1, 0, 0, 0, 0, 2),
    (1, 0, 0, 0, 0, 2),
    (0, 1, 0, 0, 2, 4),
    (-2, 0, 0, 0, 2, 4),
    (2, 0, 0, 0, 2, 4),
    (0, 1, 0, 0, 0, 2),
    (-1, 0, 0, 0, 2, 4),
    (1, 0, 0, 0, 2, 4),
]
THEN = [
    (0, 1, 0, 1, 0, 2),
    (0, 1, 0, -1, 0, 2),
    (-2, 0, 0, 1, 0, 2),
    (2, 0, 0, -1, 0, 2),
    (0, 1, 0, 2, 2, 4),
    (0, 1, 0, -2, 2, 4),
    (-1, 0, 0, 2, 2, 4),
    (1, 0, 0, -2, 2, 4),
    (-1, 0, 0, 1, 0, 2),
    (1, 0, 0, -1, 0, 2),
    (-1, 0, 1, 0, 2, 4),
    (1, 0, 1, 0, 2, 4),
    (-1, 0, 1, 1, 0, 2),
    (1, 0, 1, -1, 0, 2),
    (0, 1, 0, 3, 0, 2),
    (0, 1, 0, -3, 0, 2),
    (1, 1, 0, -3, 0, 2),
    (-1, 1, 0, 3, 2, 4),
    (-1, 0, 0, 3, 0, 2),
    (1, 0, 0, -3, 2, 4),
    (-1, 0, 1, 2, 2, 4),
    (1, 0, 1, -2, 2, 4),
    ((0, 0), (1, 0)),
    ((0, 1), (0, -1)),
    ((0, 3), (0, -3)),
    ((0, 2), (0, -2)),
    ((1, 1), (1, -1)),
    ((1, 2), (1, -2)),
    ((0, 4), (1, -3)),
    ((1, 4), (1, 3)),
]
TARGETS = sorted(
    {s[:2] for s in FIRST} | {s[:2] for s in THEN if len(s) == 6},
    key=lambda t: (-abs(t[0]) - t[1], t),
)
SENDS = FIRST + [s for s in THEN if len(s) == 6]


def wrapped(dist):
    return (dist + 3) % 8 - 3


def arrivals():
    came = {}
    for k, (up, across, plane, dist, first, end) in enumerate(SENDS):
        for part in range(first, end):
            key = ((plane + across) % 2, wrapped(dist - up), part)
            assert key not in came and key[:2] != (0, 0)
            came[key] = k
    assert len(came) == 15 * PARTS
    return came


CAME = arrivals()


def at(yy, zz, n_y):
    return lax.rem(yy + 2 * n_y, n_y) * 2 + zz


def exchange(n_y, basis_hbm, blocks, send_sem, recv_sem):
    c = lax.axis_index("cluster")
    b = lax.axis_index("blk")
    y, z = b // 2, b % 2
    sign = 1 - 2 * z
    up, down, across = at(y + sign, z, n_y), at(y - sign, z, n_y), at(y, 1 - z, n_y)

    part = basis_hbm.shape[0] // PIECES

    def copy(src, slot_at, to):
        made = []
        for k in range(PIECES):
            some = pl.ds(k * part, part)
            made.append(
                pltpu.make_async_remote_copy(
                    src_ref=basis_hbm.at[some] if src is None else blocks.at[src, some],
                    dst_ref=blocks.at[slot_at, some],
                    send_sem=send_sem.at[slot_at, k],
                    recv_sem=recv_sem.at[slot_at, k],
                    device_id=(c, to),
                    device_id_type=MESH,
                )
            )
        return made

    copies = [
        copy(None, PART, across),
        copy(None, UP, down),
        copy(None, DOWN, up),
        copy(PART, PART_UP, down),
        copy(UP, PART_DOWN, across),
        copy(PART_DOWN, PART_DOWN2, up),
    ]

    def begin():
        for k in range(PIECES):
            for slot_at in (PART, UP, DOWN):
                copies[slot_at][k].start()

    def relay():
        for k in range(PIECES):
            copies[PART][k].wait_recv()
            copies[PART_UP][k].start()
            copies[UP][k].wait_recv()
            copies[PART_DOWN][k].start()

    def relay_last():
        for k in range(PIECES):
            copies[PART_DOWN][k].wait_recv()
            copies[PART_DOWN2][k].start()

    def finish():
        for k in range(PIECES):
            for slot_at in (DOWN, PART_UP, PART_DOWN2):
                copies[slot_at][k].wait_recv()
        for k in range(PIECES):
            for slot_at in range(6):
                copies[slot_at][k].wait_send()

    return begin, relay, relay_last, finish


def gather_kernel(
    n_y, n_clust, coeff_hbm, inter_hbm, basis_hbm, coul_hbm, reach_ref,
    n_buf, w_out,
    coeff_ref, inter_ref, basis_ref, coul_v, coeff_f, out_f, out_buf, in_buf, blocks, g_ref,
    load_sem, a2a_send, a2a_recv, b_send, b_recv, ag_send, ag_recv,
):
    c = lax.axis_index("cluster")
    b = lax.axis_index("blk")
    y, z = b // 2, b % 2
    sign = 1 - 2 * z
    rows = basis_ref.shape[0]
    stops = coul_v.shape[0]
    half_stops = (stops - 1) // 2

    inter_load, coeff_load, basis_load, coul_load = [
        pltpu.make_async_copy(src, dst, load_sem.at[k])
        for k, (src, dst) in enumerate(
            (
                (inter_hbm, inter_ref),
                (coeff_hbm, coeff_ref),
                (basis_hbm, basis_ref),
                (coul_hbm, coul_v),
            )
        )
    ]
    inter_load.start()
    coeff_load.start()

    barrier = pltpu.get_barrier_semaphore()

    group = n_clust // GROUPS
    mine = c // group
    first_mate, first_later = mine * group, (mine + 1) * group

    def greet(to, _):
        pl.semaphore_signal(barrier, inc=1, device_id=(to, b), device_id_type=MESH)
        return 0

    def greet_row(rise, across):
        pl.semaphore_signal(
            barrier,
            inc=1,
            device_id=(c, at(y + rise, 1 - z if across else z, n_y)),
            device_id_type=MESH,
        )

    def greet_mate(step):
        to = first_mate + (c - first_mate + step) % group
        pl.semaphore_signal(barrier, inc=1, device_id=(to, b), device_id_type=MESH)

    middle = sorted(range(1, group), key=lambda step: (abs(step - group // 2), step))
    for step in middle[:3]:
        greet_mate(step)
    for target in TARGETS:
        if abs(target[0]) + target[1] >= 2:
            greet_row(*target)
    for step in middle[3:]:
        greet_mate(step)
    for target in TARGETS:
        if abs(target[0]) + target[1] < 2:
            greet_row(*target)
    lax.fori_loop(first_later, n_clust, greet, 0)

    inter_load.wait()
    inter = inter_ref[...]
    n_list = inter.shape[1]
    n_atoms, funcs, columns = coeff_ref.shape
    slot_rows = 2 * funcs * n_clust
    owner = inter // n_atoms
    key = lax.broadcasted_iota(jnp.int32, inter.shape, 1) * n_atoms + (inter - owner * n_atoms)
    key = key.astype(F32)
    top = F32(n_list * n_atoms)
    low = jnp.min(jnp.where(owner == c, key, top), axis=1, keepdims=True)
    high = jnp.max(jnp.where(owner == c, key, -1.0), axis=1, keepdims=True)
    low_at = jnp.where(low < top, low.astype(jnp.int32) % n_atoms, -1)
    high_at = jnp.where(high > low, high.astype(jnp.int32) % n_atoms, -1)
    atom = lax.broadcasted_iota(jnp.int32, (n_clust, n_atoms), 1)
    pick = jnp.concatenate([atom == low_at, atom == high_at], axis=0).astype(F32).astype(BF16)
    coeff_load.wait()
    coeff_f[...] = coeff_ref[...].astype(F32).reshape(n_atoms * funcs, columns)
    by_atom = jnp.concatenate(
        [coeff_f[pl.ds(m, n_atoms, stride=funcs), :].astype(BF16) for m in range(funcs)], axis=1
    )
    packed = jnp.dot(pick, by_atom, preferred_element_type=F32)
    for s in range(2):
        for m in range(funcs):
            out_f[pl.ds(s * funcs + m, n_clust, stride=2 * funcs), :] = packed[
                s * n_clust : (s + 1) * n_clust, m * columns : (m + 1) * columns
            ]
    out_buf[...] = out_f[...].astype(BF16)

    pl.semaphore_wait(barrier, first_later - 1 + len(TARGETS))

    def a2a(to, source):
        return pltpu.make_async_remote_copy(
            src_ref=out_buf.at[pl.ds(pl.multiple_of(to * 16, 16), 16)],
            dst_ref=in_buf.at[pl.ds(pl.multiple_of(source * 16, 16), 16)],
            send_sem=a2a_send.at[to],
            recv_sem=a2a_recv.at[source],
            device_id=(to, b),
            device_id_type=MESH,
        )

    def a2a_start(to, _):
        @pl.when(to != c)
        def _():
            a2a(to, c).start()

        return 0

    lax.fori_loop(0, first_later, a2a_start, 0)
    begin_basis, relay_basis, relay_basis_last, finish_basis = exchange(
        n_y, basis_hbm, blocks, b_send, b_recv
    )
    begin_basis()
    basis_load.start()
    coul_load.start()

    own_list = inter_ref[pl.ds(c, 1), :]
    own_owner = (own_list // n_atoms).astype(F32)
    entry = lax.broadcasted_iota(jnp.int32, (rows, n_list), 0) // funcs
    column = lax.broadcasted_iota(jnp.int32, (rows, n_list), 1)
    own_row = jnp.broadcast_to(own_owner, (rows, n_list))
    owner_col = jnp.sum(jnp.where(entry == column, own_row, 0.0), axis=1, keepdims=True)
    own_rank = jnp.sum(
        jnp.where((own_row == owner_col) & (column < entry), 1.0, 0.0), axis=1, keepdims=True
    )
    func_col = (lax.broadcasted_iota(jnp.int32, (rows, 1), 0) % funcs).astype(F32)
    place = owner_col * (2 * funcs) + own_rank * funcs + func_col
    unpack = (
        lax.broadcasted_iota(jnp.int32, (rows, slot_rows), 1).astype(F32) == place
    ).astype(BF16)
    own_at = pl.ds(pl.multiple_of(c * 16, 16), 16)
    in_buf[own_at, :] = out_buf[own_at, :]

    def a2a_wait(source, _):
        @pl.when(source != c)
        def _():
            a2a(c, source).wait_recv()

        return 0

    lax.fori_loop(first_mate, first_later, a2a_wait, 0)
    relay_basis()

    def answer(source, _):
        a2a(c, source).wait_recv()
        a2a(source, c).start()
        return 0

    for later in range(1, GROUPS):
        if later == GROUPS // 2:
            pl.when(mine < later)(relay_basis_last)

        @pl.when(mine < later)
        def _():
            lax.fori_loop(later * group, (later + 1) * group, answer, 0)

    pl.when(mine >= GROUPS // 2)(relay_basis_last)
    lax.fori_loop(0, first_mate, a2a_wait, 0)
    chunk = jnp.dot(unpack, in_buf[...], preferred_element_type=F32)
    n_buf[b] = chunk.astype(BF16)

    def chunk_at(plane, dist):
        return at(y + dist, z if plane == 0 else 1 - z, n_y)

    part_rows = rows // PARTS

    def send(k):
        rise, across, plane, dist, first, end = SENDS[k]
        where = n_buf.at[
            chunk_at(plane, dist), pl.ds(first * part_rows, (end - first) * part_rows)
        ]
        return pltpu.make_async_remote_copy(
            src_ref=where,
            dst_ref=where,
            send_sem=ag_send.at[k],
            recv_sem=ag_recv.at[k],
            device_id=(c, at(y + rise, 1 - z if across else z, n_y)),
            device_id_type=MESH,
        )

    have = set()

    def need(plane, dist, first=0, end=PARTS):
        if (plane, dist) == (0, 0):
            return
        for part in range(first, end):
            k = CAME[(plane, wrapped(dist), part)]
            if k not in have:
                have.add(k)
                send(k).wait_recv()

    for k in range(len(FIRST)):
        send(k).start()
    k = len(FIRST)
    folded = False

    def a2a_sent(to, _):
        @pl.when(to != c)
        def _():
            a2a(to, c).wait_send()

        return 0

    for item in THEN:
        if item == THEN[-2]:
            finish_basis()
            lax.fori_loop(0, n_clust, a2a_sent, 0)
            for j in range(len(SENDS) - LAST_SENDS):
                send(j).wait_send()
        if len(item) == 6:
            need(*item[2:])
            send(k).start()
            k += 1
        else:
            for chunk_of in item:
                need(*chunk_of)
            both = jnp.concatenate([n_buf[chunk_at(*chunk_of)] for chunk_of in item], axis=1)
            term = lax.dot_general(both, both, (((1,), (1,)), ((), ())), preferred_element_type=F32)
            g_ref[...] = g_ref[...] + term if folded else term
            folded = True

    basis_load.wait()
    basis = basis_ref[...]
    scale = (n_buf.shape[0] * n_buf.shape[2]) ** -0.5
    g = g_ref[...]
    g_hi = g.astype(BF16)
    g_lo = (g - g_hi.astype(F32)).astype(BF16)
    h = jnp.dot(basis, g_hi, preferred_element_type=F32) + jnp.dot(
        basis, g_lo, preferred_element_type=F32
    )
    h = (h * scale).astype(BF16)
    coul_load.wait()
    reach = reach_ref[0]
    w = None
    for slot_at, offset in [(None, 0)] + list(SLOT_OFFSET.items()):
        other = basis if slot_at is None else blocks[slot_at]
        density = lax.dot_general(h, other, (((1,), (1,)), ((), ())), preferred_element_type=F32)
        within = jnp.where(abs(offset) <= reach, F32(1.0), F32(0.0))
        coul = coul_v[half_stops + sign * offset].astype(F32) * within
        tile = (density * coul).astype(BF16)
        term = jnp.dot(tile, other, preferred_element_type=F32)
        w = term if w is None else w + term
    w_out[...] = w.astype(BF16)

    for k in range(len(SENDS) - LAST_SENDS, len(SENDS)):
        send(k).wait_send()


def apply_kernel(w_ref, n_ref, out_hbm, out_v, sem):
    w = w_ref[...]
    width = 4 * n_ref.shape[2]
    copies = []
    for j in range(n_ref.shape[0] // 4):
        both = jnp.concatenate([n_ref[4 * j + i] for i in range(4)], axis=1)
        where = slice(j * width, (j + 1) * width)
        out_v[:, where] = jnp.dot(w, both, preferred_element_type=F32).astype(BF16)
        copy = pltpu.make_async_copy(out_v.at[:, where], out_hbm.at[:, where], sem.at[j])
        copy.start()
        copies.append(copy)
    for copy in copies:
        copy.wait()


def solution(mesh):
    n_clust, n_blk = mesh.shape["cluster"], mesh.shape["blk"]
    n_y = n_blk // 2

    def on_device(coeff, intersection, basis_vals, coulomb, reach):
        rows, funcs = basis_vals.shape
        columns = coeff.shape[2]
        stops = coulomb.shape[1]
        vmem = pl.BlockSpec(memory_space=pltpu.VMEM)
        hbm = pl.BlockSpec(memory_space=pltpu.HBM)

        def stay(x):
            return pltpu.with_memory_space_constraint(x, pltpu.HBM)

        basis_vals = stay(basis_vals)

        def gather(*refs):
            gather_kernel(n_y, n_clust, *refs)

        needed, w = pl.pallas_call(
            gather,
            out_shape=(
                jax.ShapeDtypeStruct((n_blk, funcs, columns), BF16),
                jax.ShapeDtypeStruct((rows, funcs), BF16),
            ),
            in_specs=[hbm, hbm, hbm, hbm, pl.BlockSpec(memory_space=pltpu.SMEM)],
            out_specs=(vmem, vmem),
            scratch_shapes=[
                pltpu.VMEM(coeff.shape, BF16),
                pltpu.VMEM(intersection.shape, jnp.int32),
                pltpu.VMEM((rows, funcs), BF16),
                pltpu.VMEM((stops, rows, rows), BF16),
                pltpu.VMEM((coeff.shape[0] * coeff.shape[1], columns), F32),
                pltpu.VMEM((16 * n_clust, columns), F32),
                pltpu.VMEM((16 * n_clust, columns), BF16),
                pltpu.VMEM((16 * n_clust, columns), BF16),
                pltpu.VMEM((6, rows, funcs), BF16),
                pltpu.VMEM((funcs, funcs), F32),
                pltpu.SemaphoreType.DMA((4,)),
                pltpu.SemaphoreType.DMA((n_clust,)),
                pltpu.SemaphoreType.DMA((n_clust,)),
                pltpu.SemaphoreType.DMA((6, PIECES)),
                pltpu.SemaphoreType.DMA((6, PIECES)),
                pltpu.SemaphoreType.DMA((len(SENDS),)),
                pltpu.SemaphoreType.DMA((len(SENDS),)),
            ],
            compiler_params=pltpu.CompilerParams(
                collective_id=0, has_side_effects=True, vmem_limit_bytes=32 * 2**20
            ),
            name="gather",
        )(
            stay(coeff),
            stay(intersection),
            basis_vals,
            stay(jnp.swapaxes(coulomb, 0, 1)),
            reach,
        )

        return pl.pallas_call(
            apply_kernel,
            out_shape=jax.ShapeDtypeStruct((rows, n_blk * columns), BF16),
            in_specs=[vmem, vmem],
            out_specs=hbm,
            scratch_shapes=[
                pltpu.VMEM((rows, n_blk * columns), BF16),
                pltpu.SemaphoreType.DMA((n_blk // 2,)),
            ],
            compiler_params=pltpu.CompilerParams(vmem_limit_bytes=16 * 2**20),
            name="apply",
        )(w, needed)

    return jax.shard_map(
        on_device,
        mesh=mesh,
        in_specs=(
            P("cluster", None, "blk"),
            P(),
            P(("cluster", "blk"), None),
            P(("cluster", "blk"), None, None),
            P(("cluster", "blk")),
        ),
        out_specs=P(("cluster", "blk"), None),
        check_vma=False,
    )
```
